256 devices in a mesh: seq: 8 (over x, core), fsdp: 32 (over y, z).
Axes of the slice: x: 4, y: 4, z: 8, core: 2. Of those that a mesh axis runs over, the one named last changes fastest.
Arguments:
- queries: bfloat16 [32, 1024, 32, 128], P('fsdp', 'seq'), may hold values from -6 to 6
- keys: bfloat16 [32, 1024, 4, 128], P('fsdp', 'seq'), may hold values from -6 to 6
- values: bfloat16 [32, 1024, 4, 128], P('fsdp', 'seq'), may hold values from -6 to 6
- attn_out: bfloat16 [32, 1024, 32, 128], P('fsdp', 'seq'), may hold values from -6 to 6
- out_grad: bfloat16 [32, 1024, 5120], P('fsdp', 'seq'), may hold values from -6 to 6
- out_weight: bfloat16 [4096, 5120], P(('seq', 'fsdp')), may hold values from -0.09375 to 0.09375
- lengths: int32 [32, 3], P('fsdp'), may hold values from 1 to 512, 1024 in all within a row
Outputs:
- grad_queries: bfloat16 [32, 1024, 32, 128], P('fsdp', 'seq')
- grad_keys: bfloat16 [32, 1024, 4, 128], P('fsdp', 'seq')
- grad_values: bfloat16 [32, 1024, 4, 128], P('fsdp', 'seq')
- grad_out_weight: float32 [4096, 5120], P(('seq', 'fsdp'))
The draws below stay inside these ranges and needn't reach their ends.
Inputs may be any that keep to these rules, and one draw needn't show every extreme that they name: The 3 lengths of a pack sum to 1024; the longest has exactly 512 tokens.
All inputs are finite; a program needn't handle non-finite values.
Results may differ from the reference program's by a relative error of at most 0.02.
Values may be sent and summed in bfloat16 or wider, within the bound.
No kernel may reach another device: no remote copies, remote signals or barrier semaphores. Data moves between devices by JAX's collectives and lax.ppermute only.
A program may use at most 128 MiB of HBM per device.

```python
import math
import jax
import jax.numpy as jnp
import numpy as np
from jax import lax

D = 5120
HQ = 32
KVH = 4
HD = 128
DOCS = 3
PACK = 1024
PACKS = 32
TOKENS = 32768
N_SEQ = 8


def draw_keys(key, part):
    key = jax.random.fold_in(key, 1)
    shape = (PACKS, PACK, KVH, HD)
    base = jnp.clip(jax.random.normal(jax.random.fold_in(key, 3), shape), -6.0, 6.0)
    return base.astype(jnp.bfloat16)


def draw_queries(key, part):
    key = jax.random.fold_in(key, 2)
    shape = (PACKS, PACK, HQ, HD)
    base = jnp.clip(jax.random.normal(jax.random.fold_in(key, 6), shape), -6.0, 6.0)
    return base.astype(jnp.bfloat16)


def levels(stream_key, dims, pieces, smallest, largest):
    loudness = 1.0
    for axis_at, parts in pieces:
        heights = jax.random.uniform(jax.random.fold_in(jax.random.fold_in(stream_key, 6), axis_at), (parts,), jnp.float32, smallest / len(pieces), largest / len(pieces))
        loudness = loudness * jnp.repeat(jnp.exp(heights), dims[axis_at] // parts).reshape((-1,) + (1,) * (len(dims) - 1 - axis_at))
    return loudness


def profile(count, total, bound, skew):
    portions = [(1 << 20) // math.isqrt(grade ** skew) + 1 for grade in range(2, count + 1)]
    rest, given = total - bound - (count - 1), [1] * (count - 1)
    while rest > 0:
        candidates = [i for i in range(count - 1) if given[i] < bound]
        mass, budget = sum([portions[i] for i in candidates]), rest
        for i in candidates:
            extra = min(bound - given[i], max(1, budget * portions[i] // mass), rest)
            given[i] = given[i] + extra
            rest = rest - extra
    return np.array([bound] + given)


def uneven(key, number_of, total, bound, slope):
    if number_of == 2:
        one = jax.random.randint(key, (), max(1, total - bound), min(bound, total - 1) + 1)
        return jnp.stack([one, total - one])
    sizes = jnp.asarray(profile(number_of, total, bound, slope), jnp.int32)
    couples = (number_of - 1) // 2
    source_of, taker = sizes[1:1 + 2 * couples:2], sizes[2:2 + 2 * couples:2]
    margin = jnp.minimum(source_of - 1, bound - taker)
    shifted = jax.random.randint(jax.random.fold_in(key, 1), (couples,), 0, 1 << 20) % (margin + 1)
    sizes = sizes.at[1:1 + 2 * couples:2].set(source_of - shifted).at[2:2 + 2 * couples:2].set(taker + shifted)
    return sizes[jax.random.permutation(jax.random.fold_in(key, 2), number_of)]


def gaussian(key, extent, width, most, pieces=(), kind=jnp.bfloat16):
    factor_of = levels(key, extent, pieces, -0.22, 0.18) if pieces else 1.0
    entries = jax.random.normal(key, extent, jnp.float32) * width * factor_of
    return jnp.minimum(jnp.maximum(entries, -most), most).astype(kind)


def setup_inputs(seed: int = 0) -> dict:
    key_list = jax.random.split(jax.random.key(seed), 8)
    queries = draw_queries(jax.random.fold_in(key_list[7], 71), 0)
    keys = draw_keys(jax.random.fold_in(key_list[7], 71), 0)
    values = gaussian(key_list[2], (PACKS, PACK, KVH, HD), 1.0, 6.0, ((0, 32), (1, 8)))
    attn_out = gaussian(key_list[3], (PACKS, PACK, HQ, HD), 1.0, 6.0, ((0, 32), (1, 8)))
    out_grad = gaussian(key_list[4], (PACKS, PACK, D), 1.0, 6.0, ((0, 32), (1, 8)))
    out_weight = gaussian(key_list[5], (HQ * HD, D), (HQ * HD) ** -0.5, 0.09375, ((0, 256),))
    lengths = jax.vmap(lambda own: uneven(own, DOCS, PACK, PACK // 2, 2))(jax.random.split(key_list[6], PACKS)).reshape((PACKS, DOCS)).astype(jnp.int32)
    return dict(queries=queries, keys=keys, values=values, attn_out=attn_out, out_grad=out_grad, out_weight=out_weight, lengths=lengths)


def block_total(per_head, block_heads):
    partials = per_head.reshape(PACK, KVH, -1, block_heads, HD).sum(axis=3)
    partials = lax.optimization_barrier(partials.astype(jnp.bfloat16))
    return jnp.sum(partials.astype(jnp.float32), axis=2).astype(jnp.bfloat16)


def pack_grads(pack):
    queries, keys, values, attn_out, grad_attn, lengths = pack
    group_size = HQ // KVH
    block_heads = min(group_size, HQ // N_SEQ)
    score_scale = HD ** -0.5
    positions = jnp.arange(PACK, dtype=jnp.int32)
    doc_ends = jnp.cumsum(lengths).astype(jnp.int32)
    segment = jnp.sum((doc_ends[None, :] <= positions[:, None]).astype(jnp.int32), axis=1)
    allowed = (segment[:, None] == segment[None, :]) & (positions[None, :] <= positions[:, None])
    query_float = queries.astype(jnp.float32).reshape(PACK, KVH, group_size, HD)
    key_float = keys.astype(jnp.float32)
    value_float = values.astype(jnp.float32)
    grad_float = grad_attn.astype(jnp.float32).reshape(PACK, KVH, group_size, HD)
    out_float = attn_out.astype(jnp.float32).reshape(PACK, KVH, group_size, HD)
    scores = jnp.einsum("qcgd,kcd->cgqk", query_float, key_float) * score_scale
    masked = jnp.where(allowed, scores, -1e30)
    row_top = jnp.max(masked, axis=-1, keepdims=True)
    raised = jnp.where(allowed, jnp.exp(masked - row_top), 0.0)
    soft_rows = raised / jnp.sum(raised, axis=-1, keepdims=True)
    soft_low = soft_rows.astype(jnp.bfloat16).astype(jnp.float32)
    value_heads = jnp.einsum("cgqk,qcgd->kcgd", soft_low, grad_float)
    grad_soft = jnp.einsum("qcgd,kcd->cgqk", grad_float, value_float)
    delta = jnp.sum(grad_float * out_float, axis=-1)
    delta = jnp.transpose(delta, (1, 2, 0))[..., None]
    grad_scores = (soft_rows * (grad_soft - delta) * score_scale).astype(jnp.bfloat16).astype(jnp.float32)
    grad_queries = jnp.einsum("cgqk,kcd->qcgd", grad_scores, key_float).astype(jnp.bfloat16).reshape(PACK, HQ, HD)
    key_heads = jnp.einsum("cgqk,qcgd->kcgd", grad_scores, query_float)
    return grad_queries, block_total(key_heads, block_heads), block_total(value_heads, block_heads)


def reference(queries, keys, values, attn_out, out_grad, out_weight, lengths):
    grad_rows = out_grad.reshape(TOKENS, D)
    grad_attn = jnp.dot(grad_rows, out_weight.T, preferred_element_type=jnp.float32).astype(jnp.bfloat16)
    grad_attn = grad_attn.reshape(PACKS, PACK, HQ, HD)
    factor = TOKENS ** -0.5

    def add_pack(total, pair):
        out_pack, grad_pack = pair
        flat_out = out_pack.reshape(PACK, HQ * HD)
        term = jnp.dot(flat_out.T, grad_pack, preferred_element_type=jnp.float32) * factor
        term = lax.optimization_barrier(term.astype(jnp.bfloat16))
        return total + term.astype(jnp.float32), None

    grad_out_weight, unused = lax.scan(add_pack, jnp.zeros((HQ * HD, D), jnp.float32), (attn_out, out_grad))
    grad_queries, grad_keys, grad_values = lax.map(pack_grads, (queries, keys, values, attn_out, grad_attn, lengths))
    return grad_queries, grad_keys, grad_values, grad_out_weight
```

```python
import functools
import math

import jax
import jax.numpy as jnp
from jax import lax
from jax.experimental import pallas as pl
from jax.experimental.pallas import tpu as pltpu
from jax.sharding import Mesh
from jax.sharding import PartitionSpec as P

TOK = 128
QB = 256
PIECES = 2
F32 = jnp.float32
BF16 = jnp.bfloat16
VMEM = 56 * 1024 * 1024


def params():
    return pltpu.CompilerParams(vmem_limit_bytes=VMEM)


def shift(value, axis, by):
    size = lax.axis_size(axis)
    return lax.ppermute(value, axis, [(i, (i + by) % size) for i in range(size)])


def swap(value):
    return lax.ppermute(value, "core", [(0, 1), (1, 0)])


def weight_kernel(factor, y_first, info, own, prev, succ, far0, far1, o_own, o_sib, *outs):
    *terms, rows = outs
    here = info[0]

    def put(chip, rc, value):
        rows[pl.ds(pl.multiple_of(rc * 512 + chip * TOK, TOK), TOK), :] = value

    for rc in range(2):
        part = slice(rc * TOK, (rc + 1) * TOK)
        put(here, rc, own[part, :])
        put(lax.rem(here + 3, 4), rc, prev[part, :])
        put(lax.rem(here + 1, 4), rc, succ[part, :])
    put(lax.rem(here + 2, 4), 0, far0[...])
    put(lax.rem(here + 2, 4), 1, far1[...])
    y, z = info[1], info[2]
    low = rows[:512, :]
    high = rows[512:, :]
    for kk in range(2):
        for part in range(2):
            cols = slice(kk * 512 + part * 256, kk * 512 + part * 256 + 256)
            dims = (((0,), (0,)), ((), ()))
            term = lax.dot_general(o_own[:, cols], low, dims, preferred_element_type=F32)
            term += lax.dot_general(o_sib[:, cols], high, dims, preferred_element_type=F32)
            term = (term * factor).astype(BF16)
            for at in range(16):
                f = part * 16 + at
                ry = lax.rem(f // 8 - y + 4, 4)
                rz = lax.rem(f % 8 - z + 8, 8)
                value = term[at * 16 : at * 16 + 16, :]
                if y_first:
                    terms[0][ry, rz, kk] = value
                else:
                    terms[0][rz, ry, kk] = value


def weight_piece(y_first, info, parts, o_own, o_sib, factor):
    width = parts[0].shape[1]
    lead = (4, 8) if y_first else (8, 4)
    whole = pl.BlockSpec(memory_space=pltpu.VMEM)
    return pl.pallas_call(
        functools.partial(weight_kernel, factor, y_first),
        out_shape=(
            jax.ShapeDtypeStruct(lead + (2, 16, width), BF16),
            jax.ShapeDtypeStruct((1024, width), BF16),
        ),
        in_specs=[pl.BlockSpec(memory_space=pltpu.SMEM)] + [whole] * 7,
        out_specs=(whole, whole),
        compiler_params=params(),
        cost_estimate=pl.CostEstimate(
            flops=2 * 1024 * 1024 * width, bytes_accessed=12 * 1024 * 1024, transcendentals=0
        ),
    )(info, *parts, o_own, o_sib)


def project_kernel(info, *refs):
    *rows, weight, out = refs
    core = info[3]
    total = None
    begin = 0
    for piece in rows:
        width = piece.shape[1]
        block = weight[:, 0, :, begin : begin + width].reshape(256, width)
        term = lax.dot_general(
            piece[...], block, (((1,), (1,)), ((), ())), preferred_element_type=F32
        )
        total = term if total is None else total + term
        begin += width
    total = total.astype(out.dtype)
    for rc in range(2):
        for chip in range(4):
            at = rc * 512 + chip * TOK
            spot = chip * 256 + (core if rc == 0 else 1 - core) * TOK
            out[pl.ds(pl.multiple_of(spot, TOK), TOK), :] = total[at : at + TOK, :]


def project(info, pieces, weight, rc, dtype):
    grid_spec = pltpu.PrefetchScalarGridSpec(
        num_scalar_prefetch=1,
        grid=(2,),
        in_specs=[pl.BlockSpec(p.shape, lambda n, info: (0, 0)) for p in pieces]
        + [pl.BlockSpec((16, 1, 16, 2560), lambda n, info: (n, rc, 0, 0))],
        out_specs=pl.BlockSpec((1024, 256), lambda n, info: (0, n)),
    )
    return pl.pallas_call(
        project_kernel,
        out_shape=jax.ShapeDtypeStruct((1024, 512), dtype),
        grid_spec=grid_spec,
        compiler_params=params(),
        cost_estimate=pl.CostEstimate(
            flops=2 * 1024 * 512 * 2560, bytes_accessed=10 * 1024 * 1024, transcendentals=0
        ),
    )(info, *pieces, weight)


def attention_kernel(info, query, key, value, mine, theirs, o_own, o_sib, out, key_acc, value_acc):
    head = pl.program_id(0)
    core = info[3]
    ends = (info[4], info[4] + info[5], info[4] + info[5] + info[6])
    scale = 128 ** (-0.5)

    @pl.when(head == 0)
    def _():
        key_acc[...] = jnp.zeros_like(key_acc)
        value_acc[...] = jnp.zeros_like(value_acc)

    for block in range(4):
        at = block * QB
        begin = max(0, at - 512)
        span = at + QB - begin
        rows = slice(at, at + QB)
        cols = slice(begin, at + QB)
        q = query[rows, :]
        k = key[cols, :]
        v = value[cols, :]
        grad = (mine[rows, :].astype(F32) + theirs[rows, :].astype(F32)).astype(BF16)
        near = o_own[block * TOK : block * TOK + TOK, :].astype(F32)
        other = o_sib[block * TOK : block * TOK + TOK, :].astype(F32)
        saved = jnp.concatenate(
            [jnp.where(core == 0, near, other), jnp.where(core == 0, other, near)], axis=0
        )
        delta = jnp.sum((grad.astype(F32) * saved).T, axis=0, keepdims=True)
        i = at + lax.broadcasted_iota(jnp.int32, (1, QB), 1)
        start = jnp.zeros_like(i)
        for end in ends:
            start = jnp.where(i >= end, end, start)
        j = begin + lax.broadcasted_iota(jnp.int32, (span, QB), 0)
        scores = lax.dot_general(k, q, (((1,), (1,)), ((), ())), preferred_element_type=F32)
        scores = scores * (scale * math.log2(math.e))
        scores = jnp.where((j <= i) & (j >= start), scores, -1e30)
        top = jnp.max(scores, axis=0, keepdims=True)
        raised = jnp.exp2(scores - top)
        soft = raised * (1.0 / jnp.sum(raised, axis=0, keepdims=True))
        value_acc[cols, :] += jnp.dot(soft.astype(BF16), grad, preferred_element_type=F32)
        grad_soft = lax.dot_general(v, grad, (((1,), (1,)), ((), ())), preferred_element_type=F32)
        grad_scores = (soft * (grad_soft - delta) * scale).astype(BF16)
        key_acc[cols, :] += jnp.dot(grad_scores, q, preferred_element_type=F32)
        grad_query = lax.dot_general(
            grad_scores, k, (((0,), (0,)), ((), ())), preferred_element_type=F32
        )
        out[rows, pl.ds(pl.multiple_of(head * 128, 128), 128)] = grad_query.astype(BF16)

    @pl.when(head == 3)
    def _():
        out[:, 512:640] = key_acc[...].astype(BF16)
        out[:, 640:768] = value_acc[...].astype(BF16)


def attention(info, packed, mine, theirs, o_own, o_sib):
    grid_spec = pltpu.PrefetchScalarGridSpec(
        num_scalar_prefetch=1,
        grid=(4,),
        in_specs=[
            pl.BlockSpec((1024, 128), lambda h, info: (0, h)),
            pl.BlockSpec((1024, 128), lambda h, info: (0, 4)),
            pl.BlockSpec((1024, 128), lambda h, info: (0, 5)),
            pl.BlockSpec((1024, 128), lambda h, info: (0, h)),
            pl.BlockSpec((1024, 128), lambda h, info: (0, h)),
            pl.BlockSpec((512, 128), lambda h, info: (0, info[3] * 4 + h)),
            pl.BlockSpec((512, 128), lambda h, info: (0, info[3] * 4 + h)),
        ],
        out_specs=pl.BlockSpec((1024, 768), lambda h, info: (0, 0)),
        scratch_shapes=[pltpu.VMEM((1024, 128), F32), pltpu.VMEM((1024, 128), F32)],
    )
    return pl.pallas_call(
        attention_kernel,
        out_shape=jax.ShapeDtypeStruct((1024, 768), BF16),
        grid_spec=grid_spec,
        compiler_params=params(),
        cost_estimate=pl.CostEstimate(
            flops=4 * 10 * 256 * 256 * 128 * 10,
            bytes_accessed=8 * 1024 * 1024,
            transcendentals=4 * 10 * 256 * 256,
        ),
    )(info, packed, packed, packed, mine, theirs, o_own, o_sib)


def add(*terms):
    total = terms[0].astype(F32)
    for term in terms[1:]:
        total = total + term.astype(F32)
    return total


def ring_sum(chunks, axis):
    size = len(chunks)
    half = size // 2
    middle = chunks[half]
    cut = middle.shape[0] // 2
    up = shift(middle[:cut], axis, 1)
    down = shift(middle[cut:], axis, -1)
    for step in range(1, half):
        ahead, behind = chunks[half - step], chunks[half + step]
        if step == 1:
            ahead = jnp.concatenate([add(ahead[:cut], up).astype(BF16), ahead[cut:]], axis=0)
            behind = jnp.concatenate([behind[:cut], add(behind[cut:], down).astype(BF16)], axis=0)
        else:
            ahead = add(ahead, up).astype(BF16)
            behind = add(behind, down).astype(BF16)
        up = shift(ahead, axis, 1)
        down = shift(behind, axis, -1)
    return add(chunks[0], up, down)


def scatter_sum(term, y_first):
    first, second = ("y", "z") if y_first else ("z", "y")
    chunks = [term[r] for r in range(term.shape[0])]
    summed = ring_sum(chunks, first).astype(BF16)
    return ring_sum([summed[r] for r in range(summed.shape[0])], second)


def per_device(queries, keys, values, attn_out, out_grad, out_weight, lengths):
    x, core, y, z = (lax.axis_index(name) for name in ("x", "core", "y", "z"))
    info = jnp.stack([x, y, z, core]).astype(jnp.int32)
    info = jnp.concatenate([info, lengths[0]])
    factor = 32768 ** (-0.5)

    def halves(value):
        left, right = value[:, :2560], value[:, 2560:]
        return jnp.where(core == 0, left, right), jnp.where(core == 0, right, left)

    weight_mine, weight_theirs = halves(out_weight)
    weight_pair = jnp.stack([weight_mine, swap(weight_theirs)])
    weight = lax.all_gather(weight_pair, ("y", "z"), axis=0, tiled=False)

    o_split = jnp.transpose(attn_out.reshape(TOK, 4, 1024), (1, 0, 2))
    o_own = lax.all_to_all(o_split, "x", split_axis=0, concat_axis=0, tiled=True)
    o_own = o_own.reshape(512, 1024)
    o_sib = swap(o_own)

    grad_mine, grad_theirs = halves(out_grad[0])
    grad_chip = jnp.concatenate([grad_mine, swap(grad_theirs)], axis=0)
    width = 2560 // PIECES
    pieces, terms = [], []
    for piece in range(PIECES):
        own = grad_chip[:, piece * width : (piece + 1) * width]
        prev = shift(own, "x", 1)
        succ = shift(own, "x", -1)
        far0 = shift(prev[:TOK], "x", 1)
        far1 = shift(succ[TOK:], "x", -1)
        term, rows = weight_piece(
            piece % 2 == 0, info, (own, prev, succ, far0, far1), o_own, o_sib, factor
        )
        pieces.append(rows)
        terms.append(term)

    summed = [scatter_sum(term, piece % 2 == 0) for piece, term in enumerate(terms)]
    summed = jnp.concatenate(summed, axis=-1)
    keep = jnp.where(core == 0, summed[0], summed[1])
    give = jnp.where(core == 0, summed[1], summed[0])
    come = swap(give)
    grad_out_weight = jnp.concatenate(
        [jnp.where(core == 0, keep, come), jnp.where(core == 0, come, keep)], axis=-1
    )

    packed = jnp.concatenate(
        [
            queries.reshape(TOK, 8, 512),
            jnp.repeat(keys[0], 2, axis=1),
            jnp.repeat(values[0], 2, axis=1),
        ],
        axis=2,
    )
    packed = jnp.transpose(packed, (1, 0, 2))
    packed = lax.all_to_all(packed, ("x", "core"), split_axis=0, concat_axis=0, tiled=True)
    packed = packed.reshape(1024, 768)

    sibling_part = project(info, pieces, weight, 1, BF16)
    theirs = swap(sibling_part)
    mine = project(info, pieces, weight, 0, F32)
    grads = attention(info, packed, mine, theirs, o_own, o_sib)

    back = lax.all_to_all(
        grads.reshape(8, TOK, 768), ("x", "core"), split_axis=0, concat_axis=0, tiled=True
    )
    grad_queries = jnp.transpose(back[:, :, :512], (1, 0, 2)).reshape(1, TOK, 32, 128)

    def pair_sum(part):
        part = part.astype(F32).reshape(4, 2, TOK, 128).sum(axis=1).astype(BF16)
        return jnp.transpose(part, (1, 0, 2))[None]

    return (
        grad_queries,
        pair_sum(back[:, :, 512:640]),
        pair_sum(back[:, :, 640:768]),
        grad_out_weight,
    )


def solution(mesh):
    mesh = Mesh(mesh.devices.reshape(4, 2, 4, 8), ("x", "core", "y", "z"))
    pack, token = ("y", "z"), ("x", "core")
    placed = (
        P(pack, token, None, None),
        P(pack, token, None, None),
        P(pack, token, None, None),
        P(pack, token, None, None),
        P(pack, token, None),
        P(token + pack, None),
        P(pack, None),
    )
    return jax.shard_map(
        per_device,
        mesh=mesh,
        in_specs=placed,
        out_specs=(
            P(pack, token, None, None),
            P(pack, token, None, None),
            P(pack, token, None, None),
            P(token + pack, None),
        ),
        check_vma=False,
    )
```

```python
import functools
import math

import jax
import jax.numpy as jnp
from jax import lax
from jax.experimental import pallas as pl
from jax.experimental.pallas import tpu as pltpu
from jax.sharding import Mesh
from jax.sharding import PartitionSpec as P

TOK = 128
QB = 256
WIDTHS = (1536, 1024)
PIECES = 2
F32 = jnp.float32
BF16 = jnp.bfloat16
VMEM = 56 * 1024 * 1024
SPLIT = 1536


def params():
    return pltpu.CompilerParams(vmem_limit_bytes=VMEM)


def shift(value, axis, by):
    size = lax.axis_size(axis)
    return lax.ppermute(value, axis, [(i, (i + by) % size) for i in range(size)])


def after(value, *others):
    return lax.optimization_barrier((value, *others))[0]


def swap(value):
    return lax.ppermute(value, "core", [(0, 1), (1, 0)])


def weight_kernel(factor, absolute, info, own, prev, succ, far0, far1, o_own, o_sib, *outs):
    *terms, rows = outs
    here = info[0]

    def put(chip, rc, value):
        rows[pl.ds(pl.multiple_of(rc * 512 + chip * TOK, TOK), TOK), :] = value

    for rc in range(2):
        part = slice(rc * TOK, (rc + 1) * TOK)
        put(here, rc, own[part, :])
        put(lax.rem(here + 3, 4), rc, prev[part, :])
        put(lax.rem(here + 1, 4), rc, succ[part, :])
    put(lax.rem(here + 2, 4), 0, far0[...])
    put(lax.rem(here + 2, 4), 1, far1[...])
    y = info[1]
    low = rows[:512, :]
    high = rows[512:, :]
    for kk in range(2):
        for part in range(2):
            cols = slice(kk * 512 + part * 256, kk * 512 + part * 256 + 256)
            dims = (((0,), (0,)), ((), ()))
            term = lax.dot_general(o_own[:, cols], low, dims, preferred_element_type=F32)
            term += lax.dot_general(o_sib[:, cols], high, dims, preferred_element_type=F32)
            term = (term * factor).astype(BF16)
            for at in range(16):
                f = part * 16 + at
                ry = f // 8 if absolute else lax.rem(f // 8 - y + 4, 4)
                terms[0][ry, f % 8, kk] = term[at * 16 : at * 16 + 16, :]


def weight_piece(absolute, info, parts, o_own, o_sib, factor):
    width = parts[0].shape[1]
    whole = pl.BlockSpec(memory_space=pltpu.VMEM)
    return pl.pallas_call(
        functools.partial(weight_kernel, factor, absolute),
        out_shape=(
            jax.ShapeDtypeStruct((4, 8, 2, 16, width), BF16),
            jax.ShapeDtypeStruct((1024, width), BF16),
        ),
        in_specs=[pl.BlockSpec(memory_space=pltpu.SMEM)] + [whole] * 7,
        out_specs=(whole, whole),
        compiler_params=params(),
        cost_estimate=pl.CostEstimate(
            flops=2 * 1024 * 1024 * width, bytes_accessed=12 * 1024 * 1024, transcendentals=0
        ),
    )(info, *parts, o_own, o_sib)


def project_kernel(info, *refs):
    *inputs, out, weight = refs
    rows, near, ups, downs, up_half, down_half, rest = (
        inputs[:PIECES], inputs[PIECES], inputs[PIECES + 1 : PIECES + 4],
        inputs[PIECES + 4 : PIECES + 7], inputs[PIECES + 7], inputs[PIECES + 8], inputs[PIECES + 9],
    )
    y, z, core = info[1], info[2], info[3]

    def put(from_z, r, value):
        row = (lax.rem(y - r + 4, 4) * 8 + lax.rem(from_z + 8, 8)) * 16
        weight[pl.ds(pl.multiple_of(row, 16), 16), :SPLIT] = value

    for r in range(4):
        put(z, r, near[r, 0])
        for step in range(3):
            put(z - step - 1, r, ups[step][r, 0])
            put(z + step + 1, r, downs[step][r, 0])
        put(z + 4, r, up_half[r, 0] if r < 2 else down_half[r - 2, 0])
    weight[:, SPLIT:] = rest[...].reshape(512, 2560 - SPLIT)
    for part in range(2):
        block = slice(part * 256, part * 256 + 256)
        total = None
        begin = 0
        for piece in rows:
            width = piece.shape[1]
            term = lax.dot_general(
                piece[...],
                weight[block, begin : begin + width],
                (((1,), (1,)), ((), ())),
                preferred_element_type=F32,
            )
            total = term if total is None else total + term
            begin += width
        total = total.astype(out.dtype)
        for rc in range(2):
            for chip in range(4):
                at = rc * 512 + chip * TOK
                spot = chip * 256 + (core if rc == 0 else 1 - core) * TOK
                out[pl.ds(pl.multiple_of(spot, TOK), TOK), block] = total[at : at + TOK, :]


def project(info, pieces, parts, rest, rc, dtype):
    def half(value):
        shape = value.shape
        lead = len(shape) - 3
        block = shape[:lead] + (1,) + shape[lead + 1 :]
        return pl.BlockSpec(block, lambda n, info: (0,) * lead + (rc, 0, 0))

    grid_spec = pltpu.PrefetchScalarGridSpec(
        num_scalar_prefetch=1,
        grid=(1,),
        in_specs=[pl.BlockSpec(p.shape, lambda n, info: (0, 0)) for p in pieces]
        + [half(p) for p in parts]
        + [half(rest)],
        out_specs=pl.BlockSpec((1024, 512), lambda n, info: (0, 0)),
        scratch_shapes=[pltpu.VMEM((512, 2560), BF16)],
    )
    return pl.pallas_call(
        project_kernel,
        out_shape=jax.ShapeDtypeStruct((1024, 512), dtype),
        grid_spec=grid_spec,
        compiler_params=params(),
        cost_estimate=pl.CostEstimate(
            flops=2 * 1024 * 512 * 2560, bytes_accessed=10 * 1024 * 1024, transcendentals=0
        ),
    )(info, *pieces, *parts, rest)


def attention_kernel(info, query, key, value, mine, theirs, o_own, o_sib, out, key_acc, value_acc):
    head = pl.program_id(0)
    core = info[3]
    ends = (info[4], info[4] + info[5], info[4] + info[5] + info[6])
    scale = 128 ** (-0.5)

    @pl.when(head == 0)
    def _():
        key_acc[...] = jnp.zeros_like(key_acc)
        value_acc[...] = jnp.zeros_like(value_acc)

    for block in range(4):
        at = block * QB
        begin = max(0, at - 512)
        span = at + QB - begin
        rows = slice(at, at + QB)
        cols = slice(begin, at + QB)
        q = query[rows, :]
        k = key[cols, :]
        v = value[cols, :]
        grad = (mine[rows, :].astype(F32) + theirs[rows, :].astype(F32)).astype(BF16)
        near = o_own[block * TOK : block * TOK + TOK, :].astype(F32)
        other = o_sib[block * TOK : block * TOK + TOK, :].astype(F32)
        saved = jnp.concatenate(
            [jnp.where(core == 0, near, other), jnp.where(core == 0, other, near)], axis=0
        )
        delta = jnp.sum((grad.astype(F32) * saved).T, axis=0, keepdims=True)
        i = at + lax.broadcasted_iota(jnp.int32, (1, QB), 1)
        start = jnp.zeros_like(i)
        for end in ends:
            start = jnp.where(i >= end, end, start)
        j = begin + lax.broadcasted_iota(jnp.int32, (span, QB), 0)
        scores = lax.dot_general(k, q, (((1,), (1,)), ((), ())), preferred_element_type=F32)
        scores = scores * (scale * math.log2(math.e))
        scores = jnp.where((j <= i) & (j >= start), scores, -1e30)
        top = jnp.max(scores, axis=0, keepdims=True)
        raised = jnp.exp2(scores - top)
        soft = raised * (1.0 / jnp.sum(raised, axis=0, keepdims=True))
        value_acc[cols, :] += jnp.dot(soft.astype(BF16), grad, preferred_element_type=F32)
        grad_soft = lax.dot_general(v, grad, (((1,), (1,)), ((), ())), preferred_element_type=F32)
        grad_scores = (soft * (grad_soft - delta) * scale).astype(BF16)
        key_acc[cols, :] += jnp.dot(grad_scores, q, preferred_element_type=F32)
        grad_query = lax.dot_general(
            grad_scores, k, (((0,), (0,)), ((), ())), preferred_element_type=F32
        )
        out[rows, pl.ds(pl.multiple_of(head * 128, 128), 128)] = grad_query.astype(BF16)

    @pl.when(head == 3)
    def _():
        out[:, 512:640] = key_acc[...].astype(BF16)
        out[:, 640:768] = value_acc[...].astype(BF16)


def attention(info, packed, mine, theirs, o_own, o_sib):
    grid_spec = pltpu.PrefetchScalarGridSpec(
        num_scalar_prefetch=1,
        grid=(4,),
        in_specs=[
            pl.BlockSpec((1024, 128), lambda h, info: (0, h)),
            pl.BlockSpec((1024, 128), lambda h, info: (0, 4)),
            pl.BlockSpec((1024, 128), lambda h, info: (0, 5)),
            pl.BlockSpec((1024, 128), lambda h, info: (0, h)),
            pl.BlockSpec((1024, 128), lambda h, info: (0, h)),
            pl.BlockSpec((512, 128), lambda h, info: (0, info[3] * 4 + h)),
            pl.BlockSpec((512, 128), lambda h, info: (0, info[3] * 4 + h)),
        ],
        out_specs=pl.BlockSpec((1024, 768), lambda h, info: (0, 0)),
        scratch_shapes=[pltpu.VMEM((1024, 128), F32), pltpu.VMEM((1024, 128), F32)],
    )
    return pl.pallas_call(
        attention_kernel,
        out_shape=jax.ShapeDtypeStruct((1024, 768), BF16),
        grid_spec=grid_spec,
        compiler_params=params(),
        cost_estimate=pl.CostEstimate(
            flops=4 * 10 * 256 * 256 * 128 * 10,
            bytes_accessed=8 * 1024 * 1024,
            transcendentals=4 * 10 * 256 * 256,
        ),
    )(info, packed, packed, packed, mine, theirs, o_own, o_sib)


def add(*terms):
    total = terms[0].astype(F32)
    for term in terms[1:]:
        total = total + term.astype(F32)
    return total


def per_device(queries, keys, values, attn_out, out_grad, out_weight, lengths):
    x, core, y, z = (lax.axis_index(name) for name in ("x", "core", "y", "z"))
    info = jnp.stack([x, y, z, core]).astype(jnp.int32)
    info = jnp.concatenate([info, lengths[0]])
    factor = 32768 ** (-0.5)

    def halves(value):
        left, right = value[:, :2560], value[:, 2560:]
        return jnp.where(core == 0, left, right), jnp.where(core == 0, right, left)

    weight_mine, weight_theirs = halves(out_weight)
    weight_pair = jnp.stack([weight_mine, swap(weight_theirs)])
    head, tail = weight_pair[:, :, :SPLIT], weight_pair[:, :, SPLIT:]
    near = jnp.stack([head, shift(head, "y", 1), shift(head, "y", 2), shift(head, "y", -1)])
    rest = lax.all_gather(tail, ("y", "z"), axis=0, tiled=False)
    o_split = jnp.transpose(attn_out.reshape(TOK, 4, 1024), (1, 0, 2))
    o_own = lax.all_to_all(o_split, "x", split_axis=0, concat_axis=0, tiled=True)
    o_own = o_own.reshape(512, 1024)
    o_sib = swap(o_own)

    grad_mine, grad_theirs = halves(out_grad[0])
    grad_chip = jnp.concatenate([grad_mine, swap(grad_theirs)], axis=0)
    packed = jnp.concatenate(
        [
            queries.reshape(TOK, 8, 512),
            jnp.repeat(keys[0], 2, axis=1),
            jnp.repeat(values[0], 2, axis=1),
        ],
        axis=2,
    )
    packed = jnp.transpose(packed, (1, 0, 2))

    first_own, last_own = grad_chip[:, : WIDTHS[0]], grad_chip[:, WIDTHS[0] :]

    def weigh(absolute, parts):
        return weight_piece(absolute, info, parts, o_own, o_sib, factor)

    first_own = after(first_own, tail, near)
    prev, succ = shift(first_own, "x", 1), shift(first_own, "x", -1)
    up1, down1 = shift(near, "z", 1), shift(near, "z", -1)
    up2, down2 = shift(up1, "z", 1), shift(down1, "z", -1)
    prev, succ, up2, down2, packed = lax.optimization_barrier((prev, succ, up2, down2, packed))
    far0, far1 = shift(prev[:TOK], "x", 1), shift(succ[TOK:], "x", -1)
    up3, down3 = shift(up2, "z", 1), shift(down2, "z", -1)
    far0, far1, up3, down3, last_own = lax.optimization_barrier((far0, far1, up3, down3, last_own))
    first_term, first_rows = weigh(True, (first_own, prev, succ, far0, far1))
    prev, succ = shift(last_own, "x", 1), shift(last_own, "x", -1)
    up4, down4 = shift(up3[:2], "z", 1), shift(down3[2:], "z", -1)
    prev, succ, packed, first_term, up4, down4 = lax.optimization_barrier(
        (prev, succ, packed, first_term, up4, down4)
    )
    packed = lax.all_to_all(packed, ("x", "core"), split_axis=0, concat_axis=0, tiled=True)
    packed = packed.reshape(1024, 768)
    far0, far1 = shift(prev[:TOK], "x", 1), shift(succ[TOK:], "x", -1)
    last_term, last_rows = weigh(False, (last_own, prev, succ, far0, far1))
    terms, pieces = (first_term, last_term), (first_rows, last_rows)
    parts = (near, up1, up2, up3, down1, down2, down3, up4, down4)

    first = lax.psum_scatter(terms[0], "y", scatter_dimension=0, tiled=True)[0]
    last = terms[1]
    last = add(last[0], *(shift(last[r], "y", r) for r in (1, 2, 3))).astype(BF16)

    sibling_part = project(info, pieces, parts, rest, 1, BF16)
    theirs = swap(sibling_part)
    mine = project(info, pieces, parts, rest, 0, F32)
    grads = attention(info, packed, mine, theirs, o_own, o_sib)

    summed = after(jnp.concatenate([first, last], axis=-1), grads)
    summed = lax.psum_scatter(summed, "z", scatter_dimension=0, tiled=True)[0]
    keep = jnp.where(core == 0, summed[0], summed[1])
    give = jnp.where(core == 0, summed[1], summed[0])
    come = swap(give)
    grad_out_weight = jnp.concatenate(
        [jnp.where(core == 0, keep, come), jnp.where(core == 0, come, keep)], axis=-1
    ).astype(F32)

    back = lax.all_to_all(
        grads.reshape(8, TOK, 768), ("x", "core"), split_axis=0, concat_axis=0, tiled=True
    )
    grad_queries = jnp.transpose(back[:, :, :512], (1, 0, 2)).reshape(1, TOK, 32, 128)

    def pair_sum(part):
        part = part.astype(F32).reshape(4, 2, TOK, 128).sum(axis=1).astype(BF16)
        return jnp.transpose(part, (1, 0, 2))[None]

    return (
        grad_queries,
        pair_sum(back[:, :, 512:640]),
        pair_sum(back[:, :, 640:768]),
        grad_out_weight,
    )


def solution(mesh):
    mesh = Mesh(mesh.devices.reshape(4, 2, 4, 8), ("x", "core", "y", "z"))
    pack, token = ("y", "z"), ("x", "core")
    placed = (
        P(pack, token, None, None),
        P(pack, token, None, None),
        P(pack, token, None, None),
        P(pack, token, None, None),
        P(pack, token, None),
        P(token + pack, None),
        P(pack, None),
    )
    return jax.shard_map(
        per_device,
        mesh=mesh,
        in_specs=placed,
        out_specs=(
            P(pack, token, None, None),
            P(pack, token, None, None),
            P(pack, token, None, None),
            P(token + pack, None),
        ),
        check_vma=False,
    )
```

```python
import functools
import math

import jax
import jax.numpy as jnp
from jax import lax
from jax.experimental import pallas as pl
from jax.experimental.pallas import tpu as pltpu
from jax.sharding import Mesh
from jax.sharding import PartitionSpec as P

TOK = 128
QB = 256
WIDTHS = (1280, 1280)
PIECES = 2
F32 = jnp.float32
BF16 = jnp.bfloat16
VMEM = 56 * 1024 * 1024


def params():
    return pltpu.CompilerParams(vmem_limit_bytes=VMEM)


def shift(value, axis, by):
    size = lax.axis_size(axis)
    return lax.ppermute(value, axis, [(i, (i + by) % size) for i in range(size)])


def after(value, *others):
    return lax.optimization_barrier((value, *others))[0]


def swap(value):
    return lax.ppermute(value, "core", [(0, 1), (1, 0)])


def weight_kernel(factor, info, own, prev, succ, far0, far1, o_own, o_sib, *outs):
    *terms, rows = outs
    here = info[0]

    def put(chip, rc, value):
        rows[pl.ds(pl.multiple_of(rc * 512 + chip * TOK, TOK), TOK), :] = value

    for rc in range(2):
        part = slice(rc * TOK, (rc + 1) * TOK)
        put(here, rc, own[part, :])
        put(lax.rem(here + 3, 4), rc, prev[part, :])
        put(lax.rem(here + 1, 4), rc, succ[part, :])
    put(lax.rem(here + 2, 4), 0, far0[...])
    put(lax.rem(here + 2, 4), 1, far1[...])
    y = info[1]
    low = rows[:512, :]
    high = rows[512:, :]
    for kk in range(2):
        for part in range(2):
            cols = slice(kk * 512 + part * 256, kk * 512 + part * 256 + 256)
            dims = (((0,), (0,)), ((), ()))
            term = lax.dot_general(o_own[:, cols], low, dims, preferred_element_type=F32)
            term += lax.dot_general(o_sib[:, cols], high, dims, preferred_element_type=F32)
            term = (term * factor).astype(BF16)
            for at in range(16):
                f = part * 16 + at
                ry = lax.rem(f // 8 - y + 4, 4)
                terms[0][f % 8, ry, kk] = term[at * 16 : at * 16 + 16, :]


def weight_piece(info, parts, o_own, o_sib, factor):
    width = parts[0].shape[1]
    whole = pl.BlockSpec(memory_space=pltpu.VMEM)
    return pl.pallas_call(
        functools.partial(weight_kernel, factor),
        out_shape=(
            jax.ShapeDtypeStruct((8, 4, 2, 16, width), BF16),
            jax.ShapeDtypeStruct((1024, width), BF16),
        ),
        in_specs=[pl.BlockSpec(memory_space=pltpu.SMEM)] + [whole] * 7,
        out_specs=(whole, whole),
        compiler_params=params(),
        cost_estimate=pl.CostEstimate(
            flops=2 * 1024 * 1024 * width, bytes_accessed=12 * 1024 * 1024, transcendentals=0
        ),
    )(info, *parts, o_own, o_sib)


def project_kernel(info, *refs):
    first, last, near, prev, succ, far0, far1, out, weight = refs
    rows = (first, last)
    y, core = info[1], info[3]

    def put(from_y, at, value):
        row = lax.rem(from_y, 4) * 128 + at
        count = value.shape[0] * 16
        weight[pl.ds(pl.multiple_of(row, 64), count), :] = value.reshape(count, 2560)

    put(y, 0, near[...])
    put(y + 3, 0, prev[...])
    put(y + 1, 0, succ[...])
    put(y + 2, 0, far0[...])
    put(y + 2, 64, far1[...])
    for part in range(2):
        block = slice(part * 256, part * 256 + 256)
        total = None
        begin = 0
        for piece in rows:
            width = piece.shape[1]
            term = lax.dot_general(
                piece[...],
                weight[block, begin : begin + width],
                (((1,), (1,)), ((), ())),
                preferred_element_type=F32,
            )
            total = term if total is None else total + term
            begin += width
        total = total.astype(out.dtype)
        for rc in range(2):
            for chip in range(4):
                at = rc * 512 + chip * TOK
                spot = chip * 256 + (core if rc == 0 else 1 - core) * TOK
                out[pl.ds(pl.multiple_of(spot, TOK), TOK), block] = total[at : at + TOK, :]


def project(info, pieces, parts, rc, dtype):
    far = pl.BlockSpec((None, 4, 16, 2560), lambda n, info: (rc, 0, 0, 0))
    grid_spec = pltpu.PrefetchScalarGridSpec(
        num_scalar_prefetch=1,
        grid=(1,),
        in_specs=[pl.BlockSpec(p.shape, lambda n, info: (0, 0)) for p in pieces]
        + [pl.BlockSpec((8, 16, 2560), lambda n, info: (0, 0, 0))] * 3
        + [far, far],
        out_specs=pl.BlockSpec((1024, 512), lambda n, info: (0, 0)),
        scratch_shapes=[pltpu.VMEM((512, 2560), BF16)],
    )
    return pl.pallas_call(
        project_kernel,
        out_shape=jax.ShapeDtypeStruct((1024, 512), dtype),
        grid_spec=grid_spec,
        compiler_params=params(),
        cost_estimate=pl.CostEstimate(
            flops=2 * 1024 * 512 * 2560, bytes_accessed=10 * 1024 * 1024, transcendentals=0
        ),
    )(info, *pieces, *parts)


def attention_kernel(info, query, key, value, mine, theirs, o_own, o_sib, out, key_acc, value_acc):
    head = pl.program_id(0)
    core = info[3]
    ends = (info[4], info[4] + info[5], info[4] + info[5] + info[6])
    scale = 128 ** (-0.5)

    @pl.when(head == 0)
    def _():
        key_acc[...] = jnp.zeros_like(key_acc)
        value_acc[...] = jnp.zeros_like(value_acc)

    for block in range(4):
        at = block * QB
        begin = max(0, at - 512)
        span = at + QB - begin
        rows = slice(at, at + QB)
        cols = slice(begin, at + QB)
        q = query[rows, :]
        k = key[cols, :]
        v = value[cols, :]
        grad = (mine[rows, :].astype(F32) + theirs[rows, :].astype(F32)).astype(BF16)
        near = o_own[block * TOK : block * TOK + TOK, :].astype(F32)
        other = o_sib[block * TOK : block * TOK + TOK, :].astype(F32)
        saved = jnp.concatenate(
            [jnp.where(core == 0, near, other), jnp.where(core == 0, other, near)], axis=0
        )
        delta = jnp.sum((grad.astype(F32) * saved).T, axis=0, keepdims=True)
        i = at + lax.broadcasted_iota(jnp.int32, (1, QB), 1)
        start = jnp.zeros_like(i)
        for end in ends:
            start = jnp.where(i >= end, end, start)
        j = begin + lax.broadcasted_iota(jnp.int32, (span, QB), 0)
        scores = lax.dot_general(k, q, (((1,), (1,)), ((), ())), preferred_element_type=F32)
        scores = scores * (scale * math.log2(math.e))
        scores = jnp.where((j <= i) & (j >= start), scores, -1e30)
        top = jnp.max(scores, axis=0, keepdims=True)
        raised = jnp.exp2(scores - top)
        soft = raised * (1.0 / jnp.sum(raised, axis=0, keepdims=True))
        value_acc[cols, :] += jnp.dot(soft.astype(BF16), grad, preferred_element_type=F32)
        grad_soft = lax.dot_general(v, grad, (((1,), (1,)), ((), ())), preferred_element_type=F32)
        grad_scores = (soft * (grad_soft - delta) * scale).astype(BF16)
        key_acc[cols, :] += jnp.dot(grad_scores, q, preferred_element_type=F32)
        grad_query = lax.dot_general(
            grad_scores, k, (((0,), (0,)), ((), ())), preferred_element_type=F32
        )
        out[rows, pl.ds(pl.multiple_of(head * 128, 128), 128)] = grad_query.astype(BF16)

    @pl.when(head == 3)
    def _():
        out[:, 512:640] = key_acc[...].astype(BF16)
        out[:, 640:768] = value_acc[...].astype(BF16)


def attention(info, packed, mine, theirs, o_own, o_sib):
    grid_spec = pltpu.PrefetchScalarGridSpec(
        num_scalar_prefetch=1,
        grid=(4,),
        in_specs=[
            pl.BlockSpec((1024, 128), lambda h, info: (0, h)),
            pl.BlockSpec((1024, 128), lambda h, info: (0, 4)),
            pl.BlockSpec((1024, 128), lambda h, info: (0, 5)),
            pl.BlockSpec((1024, 128), lambda h, info: (0, h)),
            pl.BlockSpec((1024, 128), lambda h, info: (0, h)),
            pl.BlockSpec((512, 128), lambda h, info: (0, info[3] * 4 + h)),
            pl.BlockSpec((512, 128), lambda h, info: (0, info[3] * 4 + h)),
        ],
        out_specs=pl.BlockSpec((1024, 768), lambda h, info: (0, 0)),
        scratch_shapes=[pltpu.VMEM((1024, 128), F32), pltpu.VMEM((1024, 128), F32)],
    )
    return pl.pallas_call(
        attention_kernel,
        out_shape=jax.ShapeDtypeStruct((1024, 768), BF16),
        grid_spec=grid_spec,
        compiler_params=params(),
        cost_estimate=pl.CostEstimate(
            flops=4 * 10 * 256 * 256 * 128 * 10,
            bytes_accessed=8 * 1024 * 1024,
            transcendentals=4 * 10 * 256 * 256,
        ),
    )(info, packed, packed, packed, mine, theirs, o_own, o_sib)


def add(*terms):
    total = terms[0].astype(F32)
    for term in terms[1:]:
        total = total + term.astype(F32)
    return total


def per_device(queries, keys, values, attn_out, out_grad, out_weight, lengths):
    x, core, y, z = (lax.axis_index(name) for name in ("x", "core", "y", "z"))
    info = jnp.stack([x, y, z, core]).astype(jnp.int32)
    info = jnp.concatenate([info, lengths[0]])
    factor = 32768 ** (-0.5)

    def halves(value):
        left, right = value[:, :2560], value[:, 2560:]
        return jnp.where(core == 0, left, right), jnp.where(core == 0, right, left)

    weight_mine, weight_theirs = halves(out_weight)
    weight_pair = jnp.stack([weight_mine, swap(weight_theirs)])
    gathered = lax.all_gather(weight_pair, "z", axis=0, tiled=False)

    o_split = jnp.transpose(attn_out.reshape(TOK, 4, 1024), (1, 0, 2))
    o_own = lax.all_to_all(o_split, "x", split_axis=0, concat_axis=0, tiled=True)
    o_own = o_own.reshape(512, 1024)
    o_sib = swap(o_own)

    grad_mine, grad_theirs = halves(out_grad[0])
    grad_chip = jnp.concatenate([grad_mine, swap(grad_theirs)], axis=0)
    packed = jnp.concatenate(
        [
            queries.reshape(TOK, 8, 512),
            jnp.repeat(keys[0], 2, axis=1),
            jnp.repeat(values[0], 2, axis=1),
        ],
        axis=2,
    )
    packed = jnp.transpose(packed, (1, 0, 2))

    first_own, last_own = grad_chip[:, : WIDTHS[0]], grad_chip[:, WIDTHS[0] :]

    def weigh(parts):
        return weight_piece(info, parts, o_own, o_sib, factor)

    first_own = after(first_own, weight_pair)
    prev, succ = shift(first_own, "x", 1), shift(first_own, "x", -1)
    near0, near1 = gathered[:, 0], gathered[:, 1]
    prev1, succ1 = shift(near1, "y", 1), shift(near1, "y", -1)
    prev, succ, packed, near0 = lax.optimization_barrier((prev, succ, packed, near0))
    far0, far1 = shift(prev[:TOK], "x", 1), shift(succ[TOK:], "x", -1)
    far0, far1, prev1, succ1, last_own, near0 = lax.optimization_barrier(
        (far0, far1, prev1, succ1, last_own, near0)
    )
    first_term, first_rows = weigh((first_own, prev, succ, far0, far1))
    prev, succ = shift(last_own, "x", 1), shift(last_own, "x", -1)
    prev0, succ0 = shift(near0, "y", 1), shift(near0, "y", -1)
    prev, succ, packed, first_term, prev0, succ0 = lax.optimization_barrier(
        (prev, succ, packed, first_term, prev0, succ0)
    )
    packed = lax.all_to_all(packed, ("x", "core"), split_axis=0, concat_axis=0, tiled=True)
    packed = packed.reshape(1024, 768)
    far0, far1 = shift(prev[:TOK], "x", 1), shift(succ[TOK:], "x", -1)
    weight_far0 = shift(jnp.stack([prev0[:4], prev1[:4]]), "y", 1)
    weight_far1 = shift(jnp.stack([succ0[4:], succ1[4:]]), "y", -1)
    last_term, last_rows = weigh((last_own, prev, succ, far0, far1))
    pieces = (first_rows, last_rows)

    summed = [
        lax.psum_scatter(term, "z", scatter_dimension=0, tiled=True)[0]
        for term in (first_term, last_term)
    ]

    sibling_part = project(info, pieces, (near1, prev1, succ1, weight_far0, weight_far1), 1, BF16)
    theirs = swap(sibling_part)
    mine = project(info, pieces, (near0, prev0, succ0, weight_far0, weight_far1), 0, F32)
    grads = attention(info, packed, mine, theirs, o_own, o_sib)

    summed = after(jnp.concatenate(summed, axis=-1), grads)
    summed = add(summed[0], *(shift(summed[r], "y", r) for r in (1, 2, 3)))
    keep = jnp.where(core == 0, summed[0], summed[1])
    give = jnp.where(core == 0, summed[1], summed[0])
    come = swap(give)
    grad_out_weight = jnp.concatenate(
        [jnp.where(core == 0, keep, come), jnp.where(core == 0, come, keep)], axis=-1
    ).astype(F32)

    back = lax.all_to_all(
        grads.reshape(8, TOK, 768), ("x", "core"), split_axis=0, concat_axis=0, tiled=True
    )
    grad_queries = jnp.transpose(back[:, :, :512], (1, 0, 2)).reshape(1, TOK, 32, 128)

    def pair_sum(part):
        part = part.astype(F32).reshape(4, 2, TOK, 128).sum(axis=1).astype(BF16)
        return jnp.transpose(part, (1, 0, 2))[None]

    return (
        grad_queries,
        pair_sum(back[:, :, 512:640]),
        pair_sum(back[:, :, 640:768]),
        grad_out_weight,
    )


def solution(mesh):
    mesh = Mesh(mesh.devices.reshape(4, 2, 4, 8), ("x", "core", "y", "z"))
    pack, token = ("y", "z"), ("x", "core")
    placed = (
        P(pack, token, None, None),
        P(pack, token, None, None),
        P(pack, token, None, None),
        P(pack, token, None, None),
        P(pack, token, None),
        P(token + pack, None),
        P(pack, None),
    )
    return jax.shard_map(
        per_device,
        mesh=mesh,
        in_specs=placed,
        out_specs=(
            P(pack, token, None, None),
            P(pack, token, None, None),
            P(pack, token, None, None),
            P(token + pack, None),
        ),
        check_vma=False,
    )
```

```python
import functools
import math

import jax
import jax.numpy as jnp
from jax import lax
from jax.experimental import pallas as pl
from jax.experimental.pallas import tpu as pltpu
from jax.sharding import Mesh
from jax.sharding import PartitionSpec as P

TOK = 128
QB = 256
COLS = 512
F32 = jnp.float32
BF16 = jnp.bfloat16
VMEM = 56 * 1024 * 1024


def params():
    return pltpu.CompilerParams(vmem_limit_bytes=VMEM)


def shift(value, axis, by):
    size = lax.axis_size(axis)
    return lax.ppermute(value, axis, [(i, (i + by) % size) for i in range(size)])


def after(value, *others):
    return lax.optimization_barrier((value, *others))[0]


def swap(value):
    return lax.ppermute(value, "core", [(0, 1), (1, 0)])


def weight_kernel(factor, info, own, prev, succ, far0, far1, o_own, o_sib, term, rows, turned):
    here, y = info[0], info[1]

    @pl.when(pl.program_id(0) == 0)
    def _():
        turned[:, :512] = o_own[...].T
        turned[:, 512:] = o_sib[...].T

    def put(chip, rc, value):
        rows[pl.ds(pl.multiple_of(rc * 512 + chip * TOK, TOK), TOK), :] = value

    for rc in range(2):
        part = slice(rc * TOK, (rc + 1) * TOK)
        put(here, rc, own[part, :])
        put(lax.rem(here + 3, 4), rc, prev[part, :])
        put(lax.rem(here + 1, 4), rc, succ[part, :])
    put(lax.rem(here + 2, 4), 0, far0[...])
    put(lax.rem(here + 2, 4), 1, far1[...])
    for part in range(4):
        product = jnp.dot(
            turned[part * 256 : part * 256 + 256, :], rows[...], preferred_element_type=F32
        )
        product = (product * factor).astype(BF16)
        for at in range(16):
            f = part % 2 * 16 + at
            ry = lax.rem(f // 8 - y + 4, 4)
            term[f % 8, ry, part // 2] = product[at * 16 : at * 16 + 16, :]


def weight_product(info, parts, o_own, o_sib, factor):
    grid_spec = pltpu.PrefetchScalarGridSpec(
        num_scalar_prefetch=1,
        grid=(2560 // COLS,),
        in_specs=[pl.BlockSpec((p.shape[0], COLS), lambda n, info: (0, n)) for p in parts]
        + [pl.BlockSpec((512, 1024), lambda n, info: (0, 0))] * 2,
        out_specs=(
            pl.BlockSpec((8, 4, 2, 16, COLS), lambda n, info: (0, 0, 0, 0, n)),
            pl.BlockSpec((1024, COLS), lambda n, info: (0, n)),
        ),
        scratch_shapes=[pltpu.VMEM((1024, 1024), BF16)],
    )
    return pl.pallas_call(
        functools.partial(weight_kernel, factor),
        out_shape=(
            jax.ShapeDtypeStruct((8, 4, 2, 16, 2560), BF16),
            jax.ShapeDtypeStruct((1024, 2560), BF16),
        ),
        grid_spec=grid_spec,
        compiler_params=params(),
        cost_estimate=pl.CostEstimate(
            flops=2 * 1024 * 1024 * 2560, bytes_accessed=18 * 1024 * 1024, transcendentals=0
        ),
    )(info, *parts, o_own, o_sib)


def project_kernel(info, rows, block, out, weight, total):
    y, core = info[1], info[3]
    step = pl.program_id(0)
    for r in range(4):
        for z in range(8):
            row = (lax.rem(y - r + 4, 4) * 8 + z) * 16
            weight[pl.ds(pl.multiple_of(row, 16), 16), :] = block[z, r]
    product = lax.dot_general(
        rows[...], weight[...], (((1,), (1,)), ((), ())), preferred_element_type=F32
    )

    @pl.when(step == 0)
    def _():
        total[...] = product

    @pl.when(step > 0)
    def _():
        total[...] += product

    @pl.when(step == pl.num_programs(0) - 1)
    def _():
        for rc in range(2):
            for chip in range(4):
                at = rc * 512 + chip * TOK
                spot = chip * 256 + (core if rc == 0 else 1 - core) * TOK
                spot = pl.ds(pl.multiple_of(spot, TOK), TOK)
                out[spot, :] = total[at : at + TOK, :].astype(out.dtype)


def project(info, rows, weight, rc, dtype):
    grid_spec = pltpu.PrefetchScalarGridSpec(
        num_scalar_prefetch=1,
        grid=(2560 // COLS,),
        in_specs=[
            pl.BlockSpec((1024, COLS), lambda n, info: (0, n)),
            pl.BlockSpec((8, 4, None, 16, COLS), lambda n, info: (0, 0, rc, 0, n)),
        ],
        out_specs=pl.BlockSpec((1024, 512), lambda n, info: (0, 0)),
        scratch_shapes=[pltpu.VMEM((512, COLS), BF16), pltpu.VMEM((1024, 512), F32)],
    )
    return pl.pallas_call(
        project_kernel,
        out_shape=jax.ShapeDtypeStruct((1024, 512), dtype),
        grid_spec=grid_spec,
        compiler_params=params(),
        cost_estimate=pl.CostEstimate(
            flops=2 * 1024 * 512 * 2560, bytes_accessed=10 * 1024 * 1024, transcendentals=0
        ),
    )(info, rows, weight)


def attention_kernel(info, query, key, value, mine, theirs, o_own, o_sib, out, key_acc, value_acc):
    head = pl.program_id(0)
    core = info[3]
    ends = (info[4], info[4] + info[5], info[4] + info[5] + info[6])
    scale = 128 ** (-0.5)

    @pl.when(head == 0)
    def _():
        key_acc[...] = jnp.zeros_like(key_acc)
        value_acc[...] = jnp.zeros_like(value_acc)

    for block in range(4):
        at = block * QB
        begin = max(0, at - 512)
        span = at + QB - begin
        rows = slice(at, at + QB)
        cols = slice(begin, at + QB)
        q = query[rows, :]
        k = key[cols, :]
        v = value[cols, :]
        grad = (mine[rows, :].astype(F32) + theirs[rows, :].astype(F32)).astype(BF16)
        near = o_own[block * TOK : block * TOK + TOK, :].astype(F32)
        other = o_sib[block * TOK : block * TOK + TOK, :].astype(F32)
        saved = jnp.concatenate(
            [jnp.where(core == 0, near, other), jnp.where(core == 0, other, near)], axis=0
        )
        delta = jnp.sum((grad.astype(F32) * saved).T, axis=0, keepdims=True)
        i = at + lax.broadcasted_iota(jnp.int32, (1, QB), 1)
        start = jnp.zeros_like(i)
        for end in ends:
            start = jnp.where(i >= end, end, start)
        j = begin + lax.broadcasted_iota(jnp.int32, (span, QB), 0)
        scores = lax.dot_general(k, q, (((1,), (1,)), ((), ())), preferred_element_type=F32)
        scores = scores * (scale * math.log2(math.e))
        scores = jnp.where((j <= i) & (j >= start), scores, -1e30)
        top = jnp.max(scores, axis=0, keepdims=True)
        raised = jnp.exp2(scores - top)
        soft = raised * (1.0 / jnp.sum(raised, axis=0, keepdims=True))
        value_acc[cols, :] += jnp.dot(soft.astype(BF16), grad, preferred_element_type=F32)
        grad_soft = lax.dot_general(v, grad, (((1,), (1,)), ((), ())), preferred_element_type=F32)
        grad_scores = (soft * (grad_soft - delta) * scale).astype(BF16)
        key_acc[cols, :] += jnp.dot(grad_scores, q, preferred_element_type=F32)
        grad_query = lax.dot_general(
            grad_scores, k, (((0,), (0,)), ((), ())), preferred_element_type=F32
        )
        out[rows, pl.ds(pl.multiple_of(head * 128, 128), 128)] = grad_query.astype(BF16)

    @pl.when(head == 3)
    def _():
        out[:, 512:640] = key_acc[...].astype(BF16)
        out[:, 640:768] = value_acc[...].astype(BF16)


def attention(info, packed, mine, theirs, o_own, o_sib):
    grid_spec = pltpu.PrefetchScalarGridSpec(
        num_scalar_prefetch=1,
        grid=(4,),
        in_specs=[
            pl.BlockSpec((1024, 128), lambda h, info: (0, h)),
            pl.BlockSpec((1024, 128), lambda h, info: (0, 4)),
            pl.BlockSpec((1024, 128), lambda h, info: (0, 5)),
            pl.BlockSpec((1024, 128), lambda h, info: (0, h)),
            pl.BlockSpec((1024, 128), lambda h, info: (0, h)),
            pl.BlockSpec((512, 128), lambda h, info: (0, info[3] * 4 + h)),
            pl.BlockSpec((512, 128), lambda h, info: (0, info[3] * 4 + h)),
        ],
        out_specs=pl.BlockSpec((1024, 768), lambda h, info: (0, 0)),
        scratch_shapes=[pltpu.VMEM((1024, 128), F32), pltpu.VMEM((1024, 128), F32)],
    )
    return pl.pallas_call(
        attention_kernel,
        out_shape=jax.ShapeDtypeStruct((1024, 768), BF16),
        grid_spec=grid_spec,
        compiler_params=params(),
        cost_estimate=pl.CostEstimate(
            flops=14 * 10**9,
            bytes_accessed=8 * 1024 * 1024,
            transcendentals=4 * 10 * 256 * 256,
        ),
    )(info, packed, packed, packed, mine, theirs, o_own, o_sib)


def add(*terms):
    total = terms[0].astype(F32)
    for term in terms[1:]:
        total = total + term.astype(F32)
    return total


def per_device(queries, keys, values, attn_out, out_grad, out_weight, lengths):
    x, core, y, z = (lax.axis_index(name) for name in ("x", "core", "y", "z"))
    info = jnp.stack([x, y, z, core]).astype(jnp.int32)
    info = jnp.concatenate([info, lengths[0]])
    factor = 32768 ** (-0.5)

    def halves(value):
        left, right = value[:, :2560], value[:, 2560:]
        return jnp.where(core == 0, left, right), jnp.where(core == 0, right, left)

    weight_mine, weight_theirs = halves(out_weight)
    weight_pair = jnp.stack([weight_mine, swap(weight_theirs)])
    near = jnp.stack([weight_pair] + [shift(weight_pair, "y", r) for r in (1, 2, 3)])
    weight = lax.all_gather(near, "z", axis=0, tiled=False)

    o_split = jnp.transpose(attn_out.reshape(TOK, 4, 1024), (1, 0, 2))
    o_own = lax.all_to_all(o_split, "x", split_axis=0, concat_axis=0, tiled=True)
    o_own = o_own.reshape(512, 1024)
    o_sib = swap(o_own)

    grad_mine, grad_theirs = halves(out_grad[0])
    grad_chip = jnp.concatenate([grad_mine, swap(grad_theirs)], axis=0)
    packed = jnp.concatenate(
        [
            queries.reshape(TOK, 8, 512),
            jnp.repeat(keys[0], 2, axis=1),
            jnp.repeat(values[0], 2, axis=1),
        ],
        axis=2,
    )
    packed = jnp.transpose(packed, (1, 0, 2))

    own = after(grad_chip, near)
    prev, succ = shift(own, "x", 1), shift(own, "x", -1)
    prev, succ, packed = lax.optimization_barrier((prev, succ, packed))
    packed = lax.all_to_all(packed, ("x", "core"), split_axis=0, concat_axis=0, tiled=True)
    packed = packed.reshape(1024, 768)
    far0, far1 = shift(prev[:TOK], "x", 1), shift(succ[TOK:], "x", -1)
    term, rows = weight_product(info, (own, prev, succ, far0, far1), o_own, o_sib, factor)

    summed = lax.psum_scatter(term, "z", scatter_dimension=0, tiled=True)[0]

    theirs = swap(project(info, rows, weight, 1, BF16))
    mine = project(info, rows, weight, 0, F32)
    grads = attention(info, packed, mine, theirs, o_own, o_sib)
    back = lax.all_to_all(
        grads.reshape(8, TOK, 768), ("x", "core"), split_axis=0, concat_axis=0, tiled=True
    )

    summed = after(summed, back)
    summed = add(summed[0], *(shift(summed[r], "y", r) for r in (1, 2, 3)))
    keep = jnp.where(core == 0, summed[0], summed[1])
    give = jnp.where(core == 0, summed[1], summed[0])
    come = swap(give)
    grad_out_weight = jnp.concatenate(
        [jnp.where(core == 0, keep, come), jnp.where(core == 0, come, keep)], axis=-1
    ).astype(F32)

    grad_queries = jnp.transpose(back[:, :, :512], (1, 0, 2)).reshape(1, TOK, 32, 128)

    def pair_sum(part):
        part = part.astype(F32).reshape(4, 2, TOK, 128).sum(axis=1).astype(BF16)
        return jnp.transpose(part, (1, 0, 2))[None]

    return (
        grad_queries,
        pair_sum(back[:, :, 512:640]),
        pair_sum(back[:, :, 640:768]),
        grad_out_weight,
    )


def solution(mesh):
    mesh = Mesh(mesh.devices.reshape(4, 2, 4, 8), ("x", "core", "y", "z"))
    pack, token = ("y", "z"), ("x", "core")
    placed = (
        P(pack, token, None, None),
        P(pack, token, None, None),
        P(pack, token, None, None),
        P(pack, token, None, None),
        P(pack, token, None),
        P(token + pack, None),
        P(pack, None),
    )
    return jax.shard_map(
        per_device,
        mesh=mesh,
        in_specs=placed,
        out_specs=(
            P(pack, token, None, None),
            P(pack, token, None, None),
            P(pack, token, None, None),
            P(token + pack, None),
        ),
        check_vma=False,
    )
```

```python
import functools
import math

import jax
import jax.numpy as jnp
from jax import lax
from jax.experimental import pallas as pl
from jax.experimental.pallas import tpu as pltpu
from jax.sharding import Mesh
from jax.sharding import PartitionSpec as P

TOK = 128
QB = 256
COLS = 512
PCOLS = 1280
SPLIT = 3
F32 = jnp.float32
BF16 = jnp.bfloat16
VMEM = 56 * 1024 * 1024


def params():
    return pltpu.CompilerParams(vmem_limit_bytes=VMEM)


def shift(value, axis, by):
    size = lax.axis_size(axis)
    return lax.ppermute(value, axis, [(i, (i + by) % size) for i in range(size)])


def after(value, *others):
    return lax.optimization_barrier((value, *others))[0]


def swap(value):
    return lax.ppermute(value, "core", [(0, 1), (1, 0)])


def weight_kernel(factor, info, own, prev, succ, far0, far1, o_own, o_sib, *outs):
    z_first, *y_first, rows, turned, product = outs
    here, y = info[0], info[1]
    step = pl.program_id(0)

    @pl.when(step == 0)
    def _():
        turned[:, :512] = o_own[...].T
        turned[:, 512:] = o_sib[...].T

    def put(chip, rc, value):
        rows[pl.ds(pl.multiple_of(rc * 512 + chip * TOK, TOK), TOK), :] = value

    for rc in range(2):
        part = slice(rc * TOK, (rc + 1) * TOK)
        put(here, rc, own[part, :])
        put(lax.rem(here + 3, 4), rc, prev[part, :])
        put(lax.rem(here + 1, 4), rc, succ[part, :])
    put(lax.rem(here + 2, 4), 0, far0[...])
    put(lax.rem(here + 2, 4), 1, far1[...])
    for part in range(4):
        block = slice(part * 256, part * 256 + 256)
        term = jnp.dot(turned[block, :], rows[...], preferred_element_type=F32)
        product[block, :] = (term * factor).astype(BF16)

    def take(kk, r, at):
        row = kk * 512 + (lax.rem(y + r, 4) * 8 + at) * 16
        return product[pl.ds(pl.multiple_of(row, 16), 16), :]

    @pl.when(step < SPLIT)
    def _():
        for at in range(8):
            for r in range(4):
                for kk in range(2):
                    z_first[at, r, kk] = take(kk, r, at)

    @pl.when(step >= SPLIT)
    def _():
        for at in range(8):
            for r in range(4):
                for kk in range(2):
                    y_first[r][at, kk] = take(kk, r, at)


def weight_product(info, parts, o_own, o_sib, factor):
    early, late = SPLIT * COLS, 2560 - SPLIT * COLS
    grid_spec = pltpu.PrefetchScalarGridSpec(
        num_scalar_prefetch=1,
        grid=(2560 // COLS,),
        in_specs=[pl.BlockSpec((p.shape[0], COLS), lambda n, info: (0, n)) for p in parts]
        + [pl.BlockSpec((512, 1024), lambda n, info: (0, 0))] * 2,
        out_specs=(
            pl.BlockSpec(
                (8, 4, 2, 16, COLS), lambda n, info: (0, 0, 0, 0, jnp.minimum(n, SPLIT - 1))
            ),
            *[
                pl.BlockSpec((8, 2, 16, COLS), lambda n, info: (0, 0, 0, jnp.maximum(n - SPLIT, 0)))
                for _ in range(4)
            ],
            pl.BlockSpec((1024, COLS), lambda n, info: (0, n)),
        ),
        scratch_shapes=[pltpu.VMEM((1024, 1024), BF16), pltpu.VMEM((1024, COLS), BF16)],
    )
    return pl.pallas_call(
        functools.partial(weight_kernel, factor),
        out_shape=(
            jax.ShapeDtypeStruct((8, 4, 2, 16, early), BF16),
            *[jax.ShapeDtypeStruct((8, 2, 16, late), BF16) for _ in range(4)],
            jax.ShapeDtypeStruct((1024, 2560), BF16),
        ),
        grid_spec=grid_spec,
        compiler_params=params(),
        cost_estimate=pl.CostEstimate(
            flops=2 * 1024 * 1024 * 2560, bytes_accessed=18 * 1024 * 1024, transcendentals=0
        ),
    )(info, *parts, o_own, o_sib)


def project_kernel(info, rows, block, out, weight, total):
    y, core = info[1], info[3]
    step = pl.program_id(0)
    for r in range(4):
        for z in range(8):
            row = (lax.rem(y - r + 4, 4) * 8 + z) * 16
            weight[pl.ds(pl.multiple_of(row, 16), 16), :] = block[z, r]
    product = lax.dot_general(
        rows[...], weight[...], (((1,), (1,)), ((), ())), preferred_element_type=F32
    )

    @pl.when(step == 0)
    def _():
        total[...] = product

    @pl.when(step > 0)
    def _():
        total[...] += product

    @pl.when(step == pl.num_programs(0) - 1)
    def _():
        for rc in range(2):
            for chip in range(4):
                at = rc * 512 + chip * TOK
                spot = chip * 256 + (core if rc == 0 else 1 - core) * TOK
                spot = pl.ds(pl.multiple_of(spot, TOK), TOK)
                out[spot, :] = total[at : at + TOK, :].astype(out.dtype)


def project(info, rows, weight, rc, dtype):
    grid_spec = pltpu.PrefetchScalarGridSpec(
        num_scalar_prefetch=1,
        grid=(2560 // PCOLS,),
        in_specs=[
            pl.BlockSpec((1024, PCOLS), lambda n, info: (0, n)),
            pl.BlockSpec((8, 4, None, 16, PCOLS), lambda n, info: (0, 0, rc, 0, n)),
        ],
        out_specs=pl.BlockSpec((1024, 512), lambda n, info: (0, 0)),
        scratch_shapes=[pltpu.VMEM((512, PCOLS), BF16), pltpu.VMEM((1024, 512), F32)],
    )
    return pl.pallas_call(
        project_kernel,
        out_shape=jax.ShapeDtypeStruct((1024, 512), dtype),
        grid_spec=grid_spec,
        compiler_params=params(),
        cost_estimate=pl.CostEstimate(
            flops=1024 * 1024, bytes_accessed=1024 * 1024, transcendentals=0
        ),
    )(info, rows, weight)


def attention_kernel(info, query, key, value, mine, theirs, o_own, o_sib, *outs):
    *outs, out, key_acc, value_acc, turned = outs
    head = pl.program_id(0)
    here, core = info[0], info[3]
    ends = (info[4], info[4] + info[5], info[4] + info[5] + info[6])
    scale = 128 ** (-0.5)

    @pl.when(head == 0)
    def _():
        key_acc[...] = jnp.zeros_like(key_acc)
        value_acc[...] = jnp.zeros_like(value_acc)
        turned[...] = key[...].T

    for block in range(4):
        at = block * QB
        begin = max(0, at - 512)
        span = at + QB - begin
        rows = slice(at, at + QB)
        cols = slice(begin, at + QB)
        q = query[rows, :]
        k = key[cols, :]
        v = value[cols, :]
        grad = (mine[rows, :].astype(F32) + theirs[rows, :].astype(F32)).astype(BF16)
        near = o_own[block * TOK : block * TOK + TOK, :].astype(F32)
        other = o_sib[block * TOK : block * TOK + TOK, :].astype(F32)
        saved = jnp.concatenate(
            [jnp.where(core == 0, near, other), jnp.where(core == 0, other, near)], axis=0
        )
        delta = jnp.sum((grad.astype(F32) * saved).T, axis=0, keepdims=True)
        i = at + lax.broadcasted_iota(jnp.int32, (1, QB), 1)
        start = jnp.zeros_like(i)
        for end in ends:
            start = jnp.where(i >= end, end, start)
        j = begin + lax.broadcasted_iota(jnp.int32, (span, QB), 0)
        scores = lax.dot_general(k, q, (((1,), (1,)), ((), ())), preferred_element_type=F32)
        scores = jnp.where((j <= i) & (j >= start), scores, -1e30)
        top = jnp.max(scores, axis=0, keepdims=True)
        raised = jnp.exp2((scores - top) * (scale * math.log2(math.e)))
        soft = raised * (1.0 / jnp.sum(raised, axis=0, keepdims=True))
        value_acc[cols, :] += jnp.dot(soft.astype(BF16), grad, preferred_element_type=F32)
        grad_soft = lax.dot_general(v, grad, (((1,), (1,)), ((), ())), preferred_element_type=F32)
        grad_scores = (soft * (grad_soft - delta)).astype(BF16)
        key_acc[cols, :] += jnp.dot(grad_scores, q, preferred_element_type=F32)
        grad_query = jnp.dot(turned[:, cols], grad_scores, preferred_element_type=F32).T * scale
        out[rows, pl.ds(pl.multiple_of(head * 128, 128), 128)] = grad_query.astype(BF16)

    @pl.when(head == 3)
    def _():
        out[:, 512:640] = (key_acc[...] * scale).astype(BF16)
        out[:, 640:768] = value_acc[...].astype(BF16)
        for step in range(4):
            for rc in range(2):
                row = lax.rem(here + step, 4) * 256 + (core if rc == 0 else 1 - core) * TOK
                outs[step][rc] = out[pl.ds(pl.multiple_of(row, TOK), TOK), :]


def attention(info, packed, mine, theirs, o_own, o_sib):
    grid_spec = pltpu.PrefetchScalarGridSpec(
        num_scalar_prefetch=1,
        grid=(4,),
        in_specs=[
            pl.BlockSpec((1024, 128), lambda h, info: (0, h)),
            pl.BlockSpec((1024, 128), lambda h, info: (0, 4)),
            pl.BlockSpec((1024, 128), lambda h, info: (0, 5)),
            pl.BlockSpec((1024, 128), lambda h, info: (0, h)),
            pl.BlockSpec((1024, 128), lambda h, info: (0, h)),
            pl.BlockSpec((512, 128), lambda h, info: (0, info[3] * 4 + h)),
            pl.BlockSpec((512, 128), lambda h, info: (0, info[3] * 4 + h)),
        ],
        out_specs=[pl.BlockSpec((2, TOK, 768), lambda h, info: (0, 0, 0))] * 4,
        scratch_shapes=[
            pltpu.VMEM((1024, 768), BF16),
            pltpu.VMEM((1024, 128), F32),
            pltpu.VMEM((1024, 128), F32),
            pltpu.VMEM((128, 1024), BF16),
        ],
    )
    return pl.pallas_call(
        attention_kernel,
        out_shape=[jax.ShapeDtypeStruct((2, TOK, 768), BF16)] * 4,
        grid_spec=grid_spec,
        compiler_params=params(),
        cost_estimate=pl.CostEstimate(
            flops=14 * 10**9,
            bytes_accessed=8 * 1024 * 1024,
            transcendentals=4 * 10 * 256 * 256,
        ),
    )(info, packed, packed, packed, mine, theirs, o_own, o_sib)


def merge_kernel(info, *refs):
    *near, far, queries, keys, values = refs
    here, core = info[0], info[3]
    for step in range(4):
        chip = lax.rem(here - step + 4, 4)
        mine, theirs = near[step][0], far[step]
        spot = chip * 1024 + core * 512
        queries[:, pl.ds(pl.multiple_of(spot, 512), 512)] = mine[:, :512]
        spot = chip * 1024 + (1 - core) * 512
        queries[:, pl.ds(pl.multiple_of(spot, 512), 512)] = theirs[:, :512]
        both = mine[:, 512:].astype(F32) + theirs[:, 512:].astype(F32)
        spot = pl.ds(pl.multiple_of(chip * 128, 128), 128)
        keys[:, spot] = both[:, :128].astype(BF16)
        values[:, spot] = both[:, 128:].astype(BF16)


def merge(info, near, far):
    whole = pl.BlockSpec(memory_space=pltpu.VMEM)
    return pl.pallas_call(
        merge_kernel,
        out_shape=(
            jax.ShapeDtypeStruct((TOK, 4096), BF16),
            jax.ShapeDtypeStruct((TOK, 512), BF16),
            jax.ShapeDtypeStruct((TOK, 512), BF16),
        ),
        in_specs=[pl.BlockSpec(memory_space=pltpu.SMEM)] + [whole] * 5,
        out_specs=(whole, whole, whole),
        compiler_params=params(),
    )(info, *near, far)


def add(*terms):
    total = terms[0].astype(F32)
    for term in terms[1:]:
        total = total + term.astype(F32)
    return total


def per_device(queries, keys, values, attn_out, out_grad, out_weight, lengths):
    x, core, y, z = (lax.axis_index(name) for name in ("x", "core", "y", "z"))
    info = jnp.stack([x, y, z, core]).astype(jnp.int32)
    info = jnp.concatenate([info, lengths[0]])
    factor = 32768 ** (-0.5)

    def halves(value):
        left, right = value[:, :2560], value[:, 2560:]
        return jnp.where(core == 0, left, right), jnp.where(core == 0, right, left)

    weight_mine, weight_theirs = halves(out_weight)
    weight_pair = jnp.stack([weight_mine, swap(weight_theirs)])
    near = jnp.stack([weight_pair] + [shift(weight_pair, "y", r) for r in (1, 2, 3)])
    weight = lax.all_gather(near, "z", axis=0, tiled=False)

    o_split = jnp.transpose(attn_out.reshape(TOK, 4, 1024), (1, 0, 2))
    o_own = lax.all_to_all(o_split, "x", split_axis=0, concat_axis=0, tiled=True)
    o_own = o_own.reshape(512, 1024)
    o_sib = swap(o_own)

    grad_mine, grad_theirs = halves(out_grad[0])
    grad_chip = jnp.concatenate([grad_mine, swap(grad_theirs)], axis=0)
    packed = jnp.concatenate(
        [
            queries.reshape(TOK, 8, 512),
            jnp.repeat(keys[0], 2, axis=1),
            jnp.repeat(values[0], 2, axis=1),
        ],
        axis=2,
    )
    packed = jnp.transpose(packed, (1, 0, 2))

    own = after(grad_chip, near, o_own)
    prev, succ = shift(own, "x", 1), shift(own, "x", -1)
    prev, succ, packed = lax.optimization_barrier((prev, succ, packed))
    packed = lax.all_to_all(packed, ("x", "core"), split_axis=0, concat_axis=0, tiled=True)
    packed = packed.reshape(1024, 768)
    far0, far1 = shift(prev[:TOK], "x", 1), shift(succ[TOK:], "x", -1)
    z_first, *y_first, rows = weight_product(
        info, (own, prev, succ, far0, far1), o_own, o_sib, factor
    )

    z_first = lax.psum_scatter(z_first, "z", scatter_dimension=0, tiled=True)[0]
    y_first = [y_first[0]] + [shift(y_first[r], "y", r) for r in (1, 2, 3)]

    theirs = swap(project(info, rows, weight, 1, BF16))
    mine = project(info, rows, weight, 0, F32)
    grads = attention(info, packed, mine, theirs, o_own, o_sib)
    z_first = after(z_first, grads[0])
    *y_first, g0, g1, g2, g3 = lax.optimization_barrier((*y_first, *grads))

    back = [g0, shift(g1, "x", 1), shift(g2, "x", 2), shift(g3, "x", 3)]
    grad_queries, grad_keys, grad_values = merge(
        info, back, swap(jnp.stack([part[1] for part in back]))
    )

    y_first = add(*y_first).astype(BF16)
    y_first = lax.all_to_all(y_first, "z", split_axis=0, concat_axis=0, tiled=True)
    y_first = add(*(y_first[r] for r in range(8)))
    z_first = add(z_first[0], *(shift(z_first[r], "y", r) for r in (1, 2, 3)))
    summed = jnp.concatenate([z_first, y_first], axis=-1)
    keep = jnp.where(core == 0, summed[0], summed[1])
    give = jnp.where(core == 0, summed[1], summed[0])
    come = swap(give)
    grad_out_weight = jnp.concatenate(
        [jnp.where(core == 0, keep, come), jnp.where(core == 0, come, keep)], axis=-1
    ).astype(F32)

    return (
        grad_queries.reshape(1, TOK, 32, 128),
        grad_keys.reshape(1, TOK, 4, 128),
        grad_values.reshape(1, TOK, 4, 128),
        grad_out_weight,
    )


def solution(mesh):
    mesh = Mesh(mesh.devices.reshape(4, 2, 4, 8), ("x", "core", "y", "z"))
    pack, token = ("y", "z"), ("x", "core")
    placed = (
        P(pack, token, None, None),
        P(pack, token, None, None),
        P(pack, token, None, None),
        P(pack, token, None, None),
        P(pack, token, None),
        P(token + pack, None),
        P(pack, None),
    )
    return jax.shard_map(
        per_device,
        mesh=mesh,
        in_specs=placed,
        out_specs=(
            P(pack, token, None, None),
            P(pack, token, None, None),
            P(pack, token, None, None),
            P(token + pack, None),
        ),
        check_vma=False,
    )
```

```python
import functools
import math

import jax
import jax.numpy as jnp
from jax import lax
from jax.experimental import pallas as pl
from jax.experimental.pallas import tpu as pltpu
from jax.sharding import Mesh
from jax.sharding import PartitionSpec as P

TOK = 128
QB = 256
COLS = 512
PCOLS = 1280
F32 = jnp.float32
BF16 = jnp.bfloat16
VMEM = 56 * 1024 * 1024


def params():
    return pltpu.CompilerParams(vmem_limit_bytes=VMEM)


def shift(value, axis, by):
    size = lax.axis_size(axis)
    return lax.ppermute(value, axis, [(i, (i + by) % size) for i in range(size)])


def after(value, *others):
    return lax.optimization_barrier((value, *others))[0]


def swap(value):
    return lax.ppermute(value, "core", [(0, 1), (1, 0)])


def weight_kernel(factor, info, own, prev, succ, far0, far1, o_own, o_sib, term, rows, turned):
    here, y = info[0], info[1]

    @pl.when(pl.program_id(0) == 0)
    def _():
        turned[:, :512] = o_own[...].T
        turned[:, 512:] = o_sib[...].T

    def put(chip, rc, value):
        rows[pl.ds(pl.multiple_of(rc * 512 + chip * TOK, TOK), TOK), :] = value

    for rc in range(2):
        part = slice(rc * TOK, (rc + 1) * TOK)
        put(here, rc, own[part, :])
        put(lax.rem(here + 3, 4), rc, prev[part, :])
        put(lax.rem(here + 1, 4), rc, succ[part, :])
    put(lax.rem(here + 2, 4), 0, far0[...])
    put(lax.rem(here + 2, 4), 1, far1[...])
    for part in range(4):
        product = jnp.dot(
            turned[part * 256 : part * 256 + 256, :], rows[...], preferred_element_type=F32
        )
        product = (product * factor).astype(BF16)
        for at in range(16):
            f = part % 2 * 16 + at
            ry = lax.rem(f // 8 - y + 4, 4)
            term[f % 8, ry, part // 2] = product[at * 16 : at * 16 + 16, :]


def weight_product(info, parts, o_own, o_sib, factor):
    grid_spec = pltpu.PrefetchScalarGridSpec(
        num_scalar_prefetch=1,
        grid=(2560 // COLS,),
        in_specs=[pl.BlockSpec((p.shape[0], COLS), lambda n, info: (0, n)) for p in parts]
        + [pl.BlockSpec((512, 1024), lambda n, info: (0, 0))] * 2,
        out_specs=(
            pl.BlockSpec((8, 4, 2, 16, COLS), lambda n, info: (0, 0, 0, 0, n)),
            pl.BlockSpec((1024, COLS), lambda n, info: (0, n)),
        ),
        scratch_shapes=[pltpu.VMEM((1024, 1024), BF16)],
    )
    return pl.pallas_call(
        functools.partial(weight_kernel, factor),
        out_shape=(
            jax.ShapeDtypeStruct((8, 4, 2, 16, 2560), BF16),
            jax.ShapeDtypeStruct((1024, 2560), BF16),
        ),
        grid_spec=grid_spec,
        compiler_params=params(),
        cost_estimate=pl.CostEstimate(
            flops=1024 * 1024, bytes_accessed=1024 * 1024, transcendentals=0
        ),
    )(info, *parts, o_own, o_sib)


def project_kernel(info, rows, block, out, weight, total):
    y, core = info[1], info[3]
    step = pl.program_id(0)
    for r in range(4):
        for z in range(8):
            row = (lax.rem(y - r + 4, 4) * 8 + z) * 16
            weight[pl.ds(pl.multiple_of(row, 16), 16), :] = block[z, r]
    product = lax.dot_general(
        rows[...], weight[...], (((1,), (1,)), ((), ())), preferred_element_type=F32
    )

    @pl.when(step == 0)
    def _():
        total[...] = product

    @pl.when(step > 0)
    def _():
        total[...] += product

    @pl.when(step == pl.num_programs(0) - 1)
    def _():
        for rc in range(2):
            for chip in range(4):
                at = rc * 512 + chip * TOK
                spot = chip * 256 + (core if rc == 0 else 1 - core) * TOK
                spot = pl.ds(pl.multiple_of(spot, TOK), TOK)
                out[spot, :] = total[at : at + TOK, :].astype(out.dtype)


def project(info, rows, weight, rc, dtype):
    grid_spec = pltpu.PrefetchScalarGridSpec(
        num_scalar_prefetch=1,
        grid=(2560 // PCOLS,),
        in_specs=[
            pl.BlockSpec((1024, PCOLS), lambda n, info: (0, n)),
            pl.BlockSpec((8, 4, None, 16, PCOLS), lambda n, info: (0, 0, rc, 0, n)),
        ],
        out_specs=pl.BlockSpec((1024, 512), lambda n, info: (0, 0)),
        scratch_shapes=[pltpu.VMEM((512, PCOLS), BF16), pltpu.VMEM((1024, 512), F32)],
    )
    return pl.pallas_call(
        project_kernel,
        out_shape=jax.ShapeDtypeStruct((1024, 512), dtype),
        grid_spec=grid_spec,
        compiler_params=params(),
        cost_estimate=pl.CostEstimate(
            flops=1024 * 1024, bytes_accessed=1024 * 1024, transcendentals=0
        ),
    )(info, rows, weight)


def attention_kernel(info, query, key, value, mine, theirs, o_own, o_sib, *outs):
    *outs, out, key_acc, value_acc, turned = outs
    head = pl.program_id(0)
    here, core = info[0], info[3]
    ends = (info[4], info[4] + info[5], info[4] + info[5] + info[6])
    scale = 128 ** (-0.5)

    @pl.when(head == 0)
    def _():
        key_acc[...] = jnp.zeros_like(key_acc)
        value_acc[...] = jnp.zeros_like(value_acc)
        turned[...] = key[...].T

    for block in range(4):
        at = block * QB
        begin = max(0, at - 512)
        span = at + QB - begin
        rows = slice(at, at + QB)
        cols = slice(begin, at + QB)
        q = query[rows, :]
        k = key[cols, :]
        v = value[cols, :]
        grad = (mine[rows, :].astype(F32) + theirs[rows, :].astype(F32)).astype(BF16)
        near = o_own[block * TOK : block * TOK + TOK, :].astype(F32)
        other = o_sib[block * TOK : block * TOK + TOK, :].astype(F32)
        saved = jnp.concatenate(
            [jnp.where(core == 0, near, other), jnp.where(core == 0, other, near)], axis=0
        )
        delta = jnp.sum((grad.astype(F32) * saved).T, axis=0, keepdims=True)
        i = at + lax.broadcasted_iota(jnp.int32, (1, QB), 1)
        start = jnp.zeros_like(i)
        for end in ends:
            start = jnp.where(i >= end, end, start)
        j = begin + lax.broadcasted_iota(jnp.int32, (span, QB), 0)
        scores = lax.dot_general(k, q, (((1,), (1,)), ((), ())), preferred_element_type=F32)
        scores = jnp.where((j <= i) & (j >= start), scores, -1e30)
        top = jnp.max(scores, axis=0, keepdims=True)
        raised = jnp.exp2((scores - top) * (scale * math.log2(math.e)))
        soft = raised * (1.0 / jnp.sum(raised, axis=0, keepdims=True))
        value_acc[cols, :] += jnp.dot(soft.astype(BF16), grad, preferred_element_type=F32)
        grad_soft = lax.dot_general(v, grad, (((1,), (1,)), ((), ())), preferred_element_type=F32)
        grad_scores = (soft * (grad_soft - delta)).astype(BF16)
        key_acc[cols, :] += jnp.dot(grad_scores, q, preferred_element_type=F32)
        grad_query = jnp.dot(turned[:, cols], grad_scores, preferred_element_type=F32).T * scale
        out[rows, pl.ds(pl.multiple_of(head * 128, 128), 128)] = grad_query.astype(BF16)

    @pl.when(head == 3)
    def _():
        out[:, 512:640] = (key_acc[...] * scale).astype(BF16)
        out[:, 640:768] = value_acc[...].astype(BF16)
        for step in range(4):
            for rc in range(2):
                row = lax.rem(here + step, 4) * 256 + (core if rc == 0 else 1 - core) * TOK
                outs[step][rc] = out[pl.ds(pl.multiple_of(row, TOK), TOK), :]


def attention(info, packed, mine, theirs, o_own, o_sib):
    grid_spec = pltpu.PrefetchScalarGridSpec(
        num_scalar_prefetch=1,
        grid=(4,),
        in_specs=[
            pl.BlockSpec((1024, 128), lambda h, info: (0, h)),
            pl.BlockSpec((1024, 128), lambda h, info: (0, 4)),
            pl.BlockSpec((1024, 128), lambda h, info: (0, 5)),
            pl.BlockSpec((1024, 128), lambda h, info: (0, h)),
            pl.BlockSpec((1024, 128), lambda h, info: (0, h)),
            pl.BlockSpec((512, 128), lambda h, info: (0, info[3] * 4 + h)),
            pl.BlockSpec((512, 128), lambda h, info: (0, info[3] * 4 + h)),
        ],
        out_specs=[pl.BlockSpec((2, TOK, 768), lambda h, info: (0, 0, 0))] * 4,
        scratch_shapes=[
            pltpu.VMEM((1024, 768), BF16),
            pltpu.VMEM((1024, 128), F32),
            pltpu.VMEM((1024, 128), F32),
            pltpu.VMEM((128, 1024), BF16),
        ],
    )
    return pl.pallas_call(
        attention_kernel,
        out_shape=[jax.ShapeDtypeStruct((2, TOK, 768), BF16)] * 4,
        grid_spec=grid_spec,
        compiler_params=params(),
        cost_estimate=pl.CostEstimate(
            flops=14 * 10**9,
            bytes_accessed=8 * 1024 * 1024,
            transcendentals=4 * 10 * 256 * 256,
        ),
    )(info, packed, packed, packed, mine, theirs, o_own, o_sib)


def merge_kernel(info, *refs):
    *near, far, queries, keys, values = refs
    here, core = info[0], info[3]
    for step in range(4):
        chip = lax.rem(here - step + 4, 4)
        mine, theirs = near[step][0], far[step]
        spot = chip * 1024 + core * 512
        queries[:, pl.ds(pl.multiple_of(spot, 512), 512)] = mine[:, :512]
        spot = chip * 1024 + (1 - core) * 512
        queries[:, pl.ds(pl.multiple_of(spot, 512), 512)] = theirs[:, :512]
        both = mine[:, 512:].astype(F32) + theirs[:, 512:].astype(F32)
        spot = pl.ds(pl.multiple_of(chip * 128, 128), 128)
        keys[:, spot] = both[:, :128].astype(BF16)
        values[:, spot] = both[:, 128:].astype(BF16)


def merge(info, near, far):
    whole = pl.BlockSpec(memory_space=pltpu.VMEM)
    return pl.pallas_call(
        merge_kernel,
        out_shape=(
            jax.ShapeDtypeStruct((TOK, 4096), BF16),
            jax.ShapeDtypeStruct((TOK, 512), BF16),
            jax.ShapeDtypeStruct((TOK, 512), BF16),
        ),
        in_specs=[pl.BlockSpec(memory_space=pltpu.SMEM)] + [whole] * 5,
        out_specs=(whole, whole, whole),
        compiler_params=params(),
    )(info, *near, far)


def add(*terms):
    total = terms[0].astype(F32)
    for term in terms[1:]:
        total = total + term.astype(F32)
    return total


def per_device(queries, keys, values, attn_out, out_grad, out_weight, lengths):
    x, core, y, z = (lax.axis_index(name) for name in ("x", "core", "y", "z"))
    info = jnp.stack([x, y, z, core]).astype(jnp.int32)
    info = jnp.concatenate([info, lengths[0]])
    factor = 32768 ** (-0.5)

    def halves(value):
        left, right = value[:, :2560], value[:, 2560:]
        return jnp.where(core == 0, left, right), jnp.where(core == 0, right, left)

    weight_mine, weight_theirs = halves(out_weight)
    weight_pair = jnp.stack([weight_mine, swap(weight_theirs)])
    near = jnp.stack([weight_pair] + [shift(weight_pair, "y", r) for r in (1, 2, 3)])
    o_split = jnp.transpose(attn_out.reshape(TOK, 4, 1024), (1, 0, 2))
    o_own = lax.all_to_all(o_split, "x", split_axis=0, concat_axis=0, tiled=True)
    o_own = o_own.reshape(512, 1024)

    grad_mine, grad_theirs = halves(out_grad[0])
    grad_chip = jnp.concatenate([grad_mine, swap(grad_theirs)], axis=0)
    weight = lax.all_gather(after(near, grad_chip), "z", axis=0, tiled=False)

    packed = jnp.concatenate(
        [
            queries.reshape(TOK, 8, 512),
            jnp.repeat(keys[0], 2, axis=1),
            jnp.repeat(values[0], 2, axis=1),
        ],
        axis=2,
    )
    packed = jnp.transpose(packed, (1, 0, 2))

    own = after(grad_chip, weight_pair, o_split)
    prev, succ = shift(own, "x", 1), shift(own, "x", -1)
    prev, succ, packed, o_own = lax.optimization_barrier((prev, succ, packed, o_own))
    packed = lax.all_to_all(packed, ("x", "core"), split_axis=0, concat_axis=0, tiled=True)
    packed = packed.reshape(1024, 768)
    far0, far1 = shift(prev[:TOK], "x", 1), shift(succ[TOK:], "x", -1)
    o_sib = swap(o_own)
    term, rows = weight_product(info, (own, prev, succ, far0, far1), o_own, o_sib, factor)

    summed = lax.psum_scatter(term, "z", scatter_dimension=0, tiled=True)[0]

    theirs = swap(project(info, rows, weight, 1, BF16))
    mine = project(info, rows, weight, 0, F32)
    grads = attention(info, packed, mine, theirs, o_own, o_sib)

    back = [grads[0]] + [shift(grads[r], "x", r) for r in (1, 2, 3)]
    grad_queries, grad_keys, grad_values = merge(
        info, back, swap(jnp.stack([part[1] for part in back]))
    )

    summed = after(summed, *back[1:])
    summed = add(summed[0], *(shift(summed[r], "y", r) for r in (1, 2, 3)))
    keep = jnp.where(core == 0, summed[0], summed[1])
    give = jnp.where(core == 0, summed[1], summed[0])
    come = swap(give)
    grad_out_weight = jnp.concatenate(
        [jnp.where(core == 0, keep, come), jnp.where(core == 0, come, keep)], axis=-1
    ).astype(F32)

    return (
        grad_queries.reshape(1, TOK, 32, 128),
        grad_keys.reshape(1, TOK, 4, 128),
        grad_values.reshape(1, TOK, 4, 128),
        grad_out_weight,
    )


def solution(mesh):
    mesh = Mesh(mesh.devices.reshape(4, 2, 4, 8), ("x", "core", "y", "z"))
    pack, token = ("y", "z"), ("x", "core")
    placed = (
        P(pack, token, None, None),
        P(pack, token, None, None),
        P(pack, token, None, None),
        P(pack, token, None, None),
        P(pack, token, None),
        P(token + pack, None),
        P(pack, None),
    )
    return jax.shard_map(
        per_device,
        mesh=mesh,
        in_specs=placed,
        out_specs=(
            P(pack, token, None, None),
            P(pack, token, None, None),
            P(pack, token, None, None),
            P(token + pack, None),
        ),
        check_vma=False,
    )
```

```python
import functools
import math

import jax
import jax.numpy as jnp
from jax import lax
from jax.experimental import pallas as pl
from jax.experimental.pallas import tpu as pltpu
from jax.sharding import Mesh
from jax.sharding import PartitionSpec as P

TOK = 128
QB = 256
COLS = 512
PCOLS = 1280
F32 = jnp.float32
BF16 = jnp.bfloat16
VMEM = 56 * 1024 * 1024


def params():
    return pltpu.CompilerParams(vmem_limit_bytes=VMEM)


def shift(value, axis, by):
    size = lax.axis_size(axis)
    return lax.ppermute(value, axis, [(i, (i + by) % size) for i in range(size)])


def after(value, *others):
    return lax.optimization_barrier((value, *others))[0]


def swap(value):
    return lax.ppermute(value, "core", [(0, 1), (1, 0)])


def weight_kernel(factor, info, own, prev, succ, far0, far1, o_own, o_sib, term, rows, turned):
    here, y = info[0], info[1]

    @pl.when(pl.program_id(0) == 0)
    def _():
        turned[:, :512] = o_own[...].T
        turned[:, 512:] = o_sib[...].T

    def put(chip, rc, value):
        rows[pl.ds(pl.multiple_of(rc * 512 + chip * TOK, TOK), TOK), :] = value

    for rc in range(2):
        part = slice(rc * TOK, (rc + 1) * TOK)
        put(here, rc, own[part, :])
        put(lax.rem(here + 3, 4), rc, prev[part, :])
        put(lax.rem(here + 1, 4), rc, succ[part, :])
    put(lax.rem(here + 2, 4), 0, far0[...])
    put(lax.rem(here + 2, 4), 1, far1[...])
    for part in range(4):
        product = jnp.dot(
            turned[part * 256 : part * 256 + 256, :], rows[...], preferred_element_type=F32
        )
        product = (product * factor).astype(BF16)
        for at in range(16):
            f = part % 2 * 16 + at
            ry = lax.rem(f // 8 - y + 4, 4)
            term[f % 8, ry, part // 2] = product[at * 16 : at * 16 + 16, :]


def weight_product(info, parts, o_own, o_sib, factor):
    grid_spec = pltpu.PrefetchScalarGridSpec(
        num_scalar_prefetch=1,
        grid=(2560 // COLS,),
        in_specs=[pl.BlockSpec((p.shape[0], COLS), lambda n, info: (0, n)) for p in parts]
        + [pl.BlockSpec((512, 1024), lambda n, info: (0, 0))] * 2,
        out_specs=(
            pl.BlockSpec((8, 4, 2, 16, COLS), lambda n, info: (0, 0, 0, 0, n)),
            pl.BlockSpec((1024, COLS), lambda n, info: (0, n)),
        ),
        scratch_shapes=[pltpu.VMEM((1024, 1024), BF16)],
    )
    return pl.pallas_call(
        functools.partial(weight_kernel, factor),
        out_shape=(
            jax.ShapeDtypeStruct((8, 4, 2, 16, 2560), BF16),
            jax.ShapeDtypeStruct((1024, 2560), BF16),
        ),
        grid_spec=grid_spec,
        compiler_params=params(),
        cost_estimate=pl.CostEstimate(
            flops=1024 * 1024, bytes_accessed=1024 * 1024, transcendentals=0
        ),
    )(info, *parts, o_own, o_sib)


def project_kernel(info, rows, block, out, total):
    core = info[3]
    step = pl.program_id(0)
    product = lax.dot_general(
        rows[...],
        block[...].reshape(512, PCOLS),
        (((1,), (1,)), ((), ())),
        preferred_element_type=F32,
    )

    @pl.when(step == 0)
    def _():
        total[...] = product

    @pl.when(step > 0)
    def _():
        total[...] += product

    @pl.when(step == pl.num_programs(0) - 1)
    def _():
        for rc in range(2):
            for chip in range(4):
                at = rc * 512 + chip * TOK
                spot = chip * 256 + (core if rc == 0 else 1 - core) * TOK
                spot = pl.ds(pl.multiple_of(spot, TOK), TOK)
                out[spot, :] = total[at : at + TOK, :].astype(out.dtype)


def project(info, rows, weight, rc, dtype):
    grid_spec = pltpu.PrefetchScalarGridSpec(
        num_scalar_prefetch=1,
        grid=(2560 // PCOLS,),
        in_specs=[
            pl.BlockSpec((1024, PCOLS), lambda n, info: (0, n)),
            pl.BlockSpec((32, None, 16, PCOLS), lambda n, info: (0, rc, 0, n)),
        ],
        out_specs=pl.BlockSpec((1024, 512), lambda n, info: (0, 0)),
        scratch_shapes=[pltpu.VMEM((1024, 512), F32)],
    )
    return pl.pallas_call(
        project_kernel,
        out_shape=jax.ShapeDtypeStruct((1024, 512), dtype),
        grid_spec=grid_spec,
        compiler_params=params(),
        cost_estimate=pl.CostEstimate(
            flops=1024 * 1024, bytes_accessed=1024 * 1024, transcendentals=0
        ),
    )(info, rows, weight)


def attention_kernel(info, query, key, value, mine, theirs, o_own, o_sib, *outs):
    *outs, out, key_acc, value_acc, turned = outs
    head = pl.program_id(0)
    here, core = info[0], info[3]
    ends = (info[4], info[4] + info[5], info[4] + info[5] + info[6])
    scale = 128 ** (-0.5)

    @pl.when(head == 0)
    def _():
        key_acc[...] = jnp.zeros_like(key_acc)
        value_acc[...] = jnp.zeros_like(value_acc)
        turned[...] = key[...].T

    for block in range(4):
        at = block * QB
        begin = max(0, at - 512)
        span = at + QB - begin
        rows = slice(at, at + QB)
        cols = slice(begin, at + QB)
        q = query[rows, :]
        k = key[cols, :]
        v = value[cols, :]
        grad = (mine[rows, :].astype(F32) + theirs[rows, :].astype(F32)).astype(BF16)
        near = o_own[block * TOK : block * TOK + TOK, :].astype(F32)
        other = o_sib[block * TOK : block * TOK + TOK, :].astype(F32)
        saved = jnp.concatenate(
            [jnp.where(core == 0, near, other), jnp.where(core == 0, other, near)], axis=0
        )
        delta = jnp.sum((grad.astype(F32) * saved).T, axis=0, keepdims=True)
        i = at + lax.broadcasted_iota(jnp.int32, (1, QB), 1)
        start = jnp.zeros_like(i)
        for end in ends:
            start = jnp.where(i >= end, end, start)
        j = begin + lax.broadcasted_iota(jnp.int32, (span, QB), 0)
        scores = lax.dot_general(k, q, (((1,), (1,)), ((), ())), preferred_element_type=F32)
        scores = jnp.where((j <= i) & (j >= start), scores, -1e30)
        top = jnp.max(scores, axis=0, keepdims=True)
        raised = jnp.exp2((scores - top) * (scale * math.log2(math.e)))
        soft = raised * (1.0 / jnp.sum(raised, axis=0, keepdims=True))
        value_acc[cols, :] += jnp.dot(soft.astype(BF16), grad, preferred_element_type=F32)
        grad_soft = lax.dot_general(v, grad, (((1,), (1,)), ((), ())), preferred_element_type=F32)
        grad_scores = (soft * (grad_soft - delta)).astype(BF16)
        key_acc[cols, :] += jnp.dot(grad_scores, q, preferred_element_type=F32)
        grad_query = jnp.dot(turned[:, cols], grad_scores, preferred_element_type=F32).T * scale
        out[rows, pl.ds(pl.multiple_of(head * 128, 128), 128)] = grad_query.astype(BF16)

    @pl.when(head == 3)
    def _():
        out[:, 512:640] = (key_acc[...] * scale).astype(BF16)
        out[:, 640:768] = value_acc[...].astype(BF16)
        for step in range(4):
            for rc in range(2):
                row = lax.rem(here + step, 4) * 256 + (core if rc == 0 else 1 - core) * TOK
                outs[step][rc] = out[pl.ds(pl.multiple_of(row, TOK), TOK), :]


def attention(info, packed, mine, theirs, o_own, o_sib):
    grid_spec = pltpu.PrefetchScalarGridSpec(
        num_scalar_prefetch=1,
        grid=(4,),
        in_specs=[
            pl.BlockSpec((1024, 128), lambda h, info: (0, h)),
            pl.BlockSpec((1024, 128), lambda h, info: (0, 4)),
            pl.BlockSpec((1024, 128), lambda h, info: (0, 5)),
            pl.BlockSpec((1024, 128), lambda h, info: (0, h)),
            pl.BlockSpec((1024, 128), lambda h, info: (0, h)),
            pl.BlockSpec((512, 128), lambda h, info: (0, info[3] * 4 + h)),
            pl.BlockSpec((512, 128), lambda h, info: (0, info[3] * 4 + h)),
        ],
        out_specs=[pl.BlockSpec((2, TOK, 768), lambda h, info: (0, 0, 0))] * 4,
        scratch_shapes=[
            pltpu.VMEM((1024, 768), BF16),
            pltpu.VMEM((1024, 128), F32),
            pltpu.VMEM((1024, 128), F32),
            pltpu.VMEM((128, 1024), BF16),
        ],
    )
    return pl.pallas_call(
        attention_kernel,
        out_shape=[jax.ShapeDtypeStruct((2, TOK, 768), BF16)] * 4,
        grid_spec=grid_spec,
        compiler_params=params(),
        cost_estimate=pl.CostEstimate(
            flops=14 * 10**9,
            bytes_accessed=8 * 1024 * 1024,
            transcendentals=4 * 10 * 256 * 256,
        ),
    )(info, packed, packed, packed, mine, theirs, o_own, o_sib)


def merge_kernel(info, *refs):
    *near, far, queries, keys, values = refs
    here, core = info[0], info[3]
    for step in range(4):
        chip = lax.rem(here - step + 4, 4)
        mine, theirs = near[step][0], far[step]
        spot = chip * 1024 + core * 512
        queries[:, pl.ds(pl.multiple_of(spot, 512), 512)] = mine[:, :512]
        spot = chip * 1024 + (1 - core) * 512
        queries[:, pl.ds(pl.multiple_of(spot, 512), 512)] = theirs[:, :512]
        both = mine[:, 512:].astype(F32) + theirs[:, 512:].astype(F32)
        spot = pl.ds(pl.multiple_of(chip * 128, 128), 128)
        keys[:, spot] = both[:, :128].astype(BF16)
        values[:, spot] = both[:, 128:].astype(BF16)


def merge(info, near, far):
    whole = pl.BlockSpec(memory_space=pltpu.VMEM)
    return pl.pallas_call(
        merge_kernel,
        out_shape=(
            jax.ShapeDtypeStruct((TOK, 4096), BF16),
            jax.ShapeDtypeStruct((TOK, 512), BF16),
            jax.ShapeDtypeStruct((TOK, 512), BF16),
        ),
        in_specs=[pl.BlockSpec(memory_space=pltpu.SMEM)] + [whole] * 5,
        out_specs=(whole, whole, whole),
        compiler_params=params(),
    )(info, *near, far)


def add(*terms):
    total = terms[0].astype(F32)
    for term in terms[1:]:
        total = total + term.astype(F32)
    return total


def per_device(queries, keys, values, attn_out, out_grad, out_weight, lengths):
    x, core, y, z = (lax.axis_index(name) for name in ("x", "core", "y", "z"))
    info = jnp.stack([x, y, z, core]).astype(jnp.int32)
    info = jnp.concatenate([info, lengths[0]])
    factor = 32768 ** (-0.5)

    def halves(value):
        left, right = value[:, :2560], value[:, 2560:]
        return jnp.where(core == 0, left, right), jnp.where(core == 0, right, left)

    weight_mine, weight_theirs = halves(out_weight)
    weight_pair = jnp.stack([weight_mine, swap(weight_theirs)])
    weight = lax.all_gather(weight_pair, ("y", "z"), axis=0, tiled=False)

    o_split = jnp.transpose(attn_out.reshape(TOK, 4, 1024), (1, 0, 2))
    o_own = lax.all_to_all(o_split, "x", split_axis=0, concat_axis=0, tiled=True)
    o_own = o_own.reshape(512, 1024)

    grad_mine, grad_theirs = halves(out_grad[0])
    grad_chip = jnp.concatenate([grad_mine, swap(grad_theirs)], axis=0)
    packed = jnp.concatenate(
        [
            queries.reshape(TOK, 8, 512),
            jnp.repeat(keys[0], 2, axis=1),
            jnp.repeat(values[0], 2, axis=1),
        ],
        axis=2,
    )
    packed = jnp.transpose(packed, (1, 0, 2))

    own = after(grad_chip, weight_pair, o_split)
    prev, succ = shift(own, "x", 1), shift(own, "x", -1)
    prev, succ, packed, o_own = lax.optimization_barrier((prev, succ, packed, o_own))
    packed = lax.all_to_all(packed, ("x", "core"), split_axis=0, concat_axis=0, tiled=True)
    packed = packed.reshape(1024, 768)
    far0, far1 = shift(prev[:TOK], "x", 1), shift(succ[TOK:], "x", -1)
    o_sib = swap(o_own)
    term, rows = weight_product(info, (own, prev, succ, far0, far1), o_own, o_sib, factor)

    summed = lax.psum_scatter(term, "z", scatter_dimension=0, tiled=True)[0]

    theirs = swap(project(info, rows, weight, 1, BF16))
    mine = project(info, rows, weight, 0, F32)
    grads = attention(info, packed, mine, theirs, o_own, o_sib)

    back = [grads[0]] + [shift(grads[r], "x", r) for r in (1, 2, 3)]
    grad_queries, grad_keys, grad_values = merge(
        info, back, swap(jnp.stack([part[1] for part in back]))
    )

    summed = after(summed, *back[1:])
    summed = add(summed[0], *(shift(summed[r], "y", r) for r in (1, 2, 3)))
    keep = jnp.where(core == 0, summed[0], summed[1])
    give = jnp.where(core == 0, summed[1], summed[0])
    come = swap(give)
    grad_out_weight = jnp.concatenate(
        [jnp.where(core == 0, keep, come), jnp.where(core == 0, come, keep)], axis=-1
    ).astype(F32)

    return (
        grad_queries.reshape(1, TOK, 32, 128),
        grad_keys.reshape(1, TOK, 4, 128),
        grad_values.reshape(1, TOK, 4, 128),
        grad_out_weight,
    )


def solution(mesh):
    mesh = Mesh(mesh.devices.reshape(4, 2, 4, 8), ("x", "core", "y", "z"))
    pack, token = ("y", "z"), ("x", "core")
    placed = (
        P(pack, token, None, None),
        P(pack, token, None, None),
        P(pack, token, None, None),
        P(pack, token, None, None),
        P(pack, token, None),
        P(token + pack, None),
        P(pack, None),
    )
    return jax.shard_map(
        per_device,
        mesh=mesh,
        in_specs=placed,
        out_specs=(
            P(pack, token, None, None),
            P(pack, token, None, None),
            P(pack, token, None, None),
            P(token + pack, None),
        ),
        check_vma=False,
    )
```

```python
import functools
import math

import jax
import jax.numpy as jnp
from jax import lax
from jax.experimental import pallas as pl
from jax.experimental.pallas import tpu as pltpu
from jax.sharding import Mesh
from jax.sharding import PartitionSpec as P

TOK = 128
QB = 256
COLS = 512
PCOLS = 1280
F32 = jnp.float32
BF16 = jnp.bfloat16
VMEM = 56 * 1024 * 1024


def params():
    return pltpu.CompilerParams(vmem_limit_bytes=VMEM)


def shift(value, axis, by):
    size = lax.axis_size(axis)
    return lax.ppermute(value, axis, [(i, (i + by) % size) for i in range(size)])


def after(value, *others):
    return lax.optimization_barrier((value, *others))[0]


def swap(value):
    return lax.ppermute(value, "core", [(0, 1), (1, 0)])


def turn_kernel(o_own, o_sib, turned):
    turned[:, :512] = o_own[...].T
    turned[:, 512:] = o_sib[...].T


def turn(o_own, o_sib):
    whole = pl.BlockSpec(memory_space=pltpu.VMEM)
    return pl.pallas_call(
        turn_kernel,
        out_shape=jax.ShapeDtypeStruct((1024, 1024), BF16),
        in_specs=[whole, whole],
        out_specs=whole,
        compiler_params=params(),
    )(o_own, o_sib)


def weight_kernel(factor, info, *refs):
    *parts, turned, term, rows = refs
    here, y = info[0], info[1]
    for place, (chip, rc) in enumerate((step, rc) for step in (0, 3, 1, 2) for rc in range(2)):
        spot = rc * 512 + lax.rem(here + chip, 4) * TOK
        rows[pl.ds(pl.multiple_of(spot, TOK), TOK), :] = parts[place][...]
    for part in range(4):
        product = jnp.dot(
            turned[part * 256 : part * 256 + 256, :], rows[...], preferred_element_type=F32
        )
        product = (product * factor).astype(BF16)
        for at in range(16):
            f = part % 2 * 16 + at
            ry = lax.rem(f // 8 - y + 4, 4)
            term[f % 8, ry, part // 2] = product[at * 16 : at * 16 + 16, :]


def weight_product(info, parts, turned, factor):
    grid_spec = pltpu.PrefetchScalarGridSpec(
        num_scalar_prefetch=1,
        grid=(2560 // COLS,),
        in_specs=[pl.BlockSpec((p.shape[0], COLS), lambda n, info: (0, n)) for p in parts]
        + [pl.BlockSpec((1024, 1024), lambda n, info: (0, 0))],
        out_specs=(
            pl.BlockSpec((8, 4, 2, 16, COLS), lambda n, info: (0, 0, 0, 0, n)),
            pl.BlockSpec((1024, COLS), lambda n, info: (0, n)),
        ),
    )
    return pl.pallas_call(
        functools.partial(weight_kernel, factor),
        out_shape=(
            jax.ShapeDtypeStruct((8, 4, 2, 16, 2560), BF16),
            jax.ShapeDtypeStruct((1024, 2560), BF16),
        ),
        grid_spec=grid_spec,
        compiler_params=params(),
        cost_estimate=pl.CostEstimate(
            flops=1024 * 1024, bytes_accessed=1024 * 1024, transcendentals=0
        ),
    )(info, *parts, turned)


def project_kernel(info, rows, block, out, weight, total):
    y, core = info[1], info[3]
    step = pl.program_id(0)
    for r in range(4):
        for z in range(8):
            row = (lax.rem(y - r + 4, 4) * 8 + z) * 16
            weight[pl.ds(pl.multiple_of(row, 16), 16), :] = block[z, r]
    product = lax.dot_general(
        rows[...], weight[...], (((1,), (1,)), ((), ())), preferred_element_type=F32
    )

    @pl.when(step == 0)
    def _():
        total[...] = product

    @pl.when(step > 0)
    def _():
        total[...] += product

    @pl.when(step == pl.num_programs(0) - 1)
    def _():
        for rc in range(2):
            for chip in range(4):
                at = rc * 512 + chip * TOK
                spot = chip * 256 + (core if rc == 0 else 1 - core) * TOK
                spot = pl.ds(pl.multiple_of(spot, TOK), TOK)
                out[spot, :] = total[at : at + TOK, :].astype(out.dtype)


def project(info, rows, weight, rc, dtype):
    grid_spec = pltpu.PrefetchScalarGridSpec(
        num_scalar_prefetch=1,
        grid=(2560 // PCOLS,),
        in_specs=[
            pl.BlockSpec((1024, PCOLS), lambda n, info: (0, n)),
            pl.BlockSpec((8, 4, None, 16, PCOLS), lambda n, info: (0, 0, rc, 0, n)),
        ],
        out_specs=pl.BlockSpec((1024, 512), lambda n, info: (0, 0)),
        scratch_shapes=[pltpu.VMEM((512, PCOLS), BF16), pltpu.VMEM((1024, 512), F32)],
    )
    return pl.pallas_call(
        project_kernel,
        out_shape=jax.ShapeDtypeStruct((1024, 512), dtype),
        grid_spec=grid_spec,
        compiler_params=params(),
        cost_estimate=pl.CostEstimate(
            flops=1024 * 1024, bytes_accessed=1024 * 1024, transcendentals=0
        ),
    )(info, rows, weight)


def attention_kernel(info, query, key, value, mine, theirs, o_own, o_sib, *outs):
    *outs, out, key_acc, value_acc, turned = outs
    head = pl.program_id(0)
    here, core = info[0], info[3]
    ends = (info[4], info[4] + info[5], info[4] + info[5] + info[6])
    scale = 128 ** (-0.5)

    @pl.when(head == 0)
    def _():
        key_acc[...] = jnp.zeros_like(key_acc)
        value_acc[...] = jnp.zeros_like(value_acc)
        turned[...] = key[...].T

    for block in range(4):
        at = block * QB
        begin = max(0, at - 512)
        span = at + QB - begin
        rows = slice(at, at + QB)
        cols = slice(begin, at + QB)
        q = query[rows, :]
        k = key[cols, :]
        v = value[cols, :]
        grad = (mine[rows, :].astype(F32) + theirs[rows, :].astype(F32)).astype(BF16)
        near = o_own[block * TOK : block * TOK + TOK, :].astype(F32)
        other = o_sib[block * TOK : block * TOK + TOK, :].astype(F32)
        saved = jnp.concatenate(
            [jnp.where(core == 0, near, other), jnp.where(core == 0, other, near)], axis=0
        )
        delta = jnp.sum((grad.astype(F32) * saved).T, axis=0, keepdims=True)
        i = at + lax.broadcasted_iota(jnp.int32, (1, QB), 1)
        start = jnp.zeros_like(i)
        for end in ends:
            start = jnp.where(i >= end, end, start)
        j = begin + lax.broadcasted_iota(jnp.int32, (span, QB), 0)
        scores = lax.dot_general(k, q, (((1,), (1,)), ((), ())), preferred_element_type=F32)
        scores = jnp.where((j <= i) & (j >= start), scores, -1e30)
        top = jnp.max(scores, axis=0, keepdims=True)
        raised = jnp.exp2((scores - top) * (scale * math.log2(math.e)))
        soft = raised * (1.0 / jnp.sum(raised, axis=0, keepdims=True))
        value_acc[cols, :] += jnp.dot(soft.astype(BF16), grad, preferred_element_type=F32)
        grad_soft = lax.dot_general(v, grad, (((1,), (1,)), ((), ())), preferred_element_type=F32)
        grad_scores = (soft * (grad_soft - delta)).astype(BF16)
        key_acc[cols, :] += jnp.dot(grad_scores, q, preferred_element_type=F32)
        grad_query = jnp.dot(turned[:, cols], grad_scores, preferred_element_type=F32).T * scale
        out[rows, pl.ds(pl.multiple_of(head * 128, 128), 128)] = grad_query.astype(BF16)

    @pl.when(head == 3)
    def _():
        out[:, 512:640] = (key_acc[...] * scale).astype(BF16)
        out[:, 640:768] = value_acc[...].astype(BF16)
        for step in range(4):
            for rc in range(2):
                row = lax.rem(here + step, 4) * 256 + (core if rc == 0 else 1 - core) * TOK
                outs[step][rc] = out[pl.ds(pl.multiple_of(row, TOK), TOK), :]


def attention(info, packed, mine, theirs, o_own, o_sib):
    grid_spec = pltpu.PrefetchScalarGridSpec(
        num_scalar_prefetch=1,
        grid=(4,),
        in_specs=[
            pl.BlockSpec((1024, 128), lambda h, info: (0, h)),
            pl.BlockSpec((1024, 128), lambda h, info: (0, 4)),
            pl.BlockSpec((1024, 128), lambda h, info: (0, 5)),
            pl.BlockSpec((1024, 128), lambda h, info: (0, h)),
            pl.BlockSpec((1024, 128), lambda h, info: (0, h)),
            pl.BlockSpec((512, 128), lambda h, info: (0, info[3] * 4 + h)),
            pl.BlockSpec((512, 128), lambda h, info: (0, info[3] * 4 + h)),
        ],
        out_specs=[pl.BlockSpec((2, TOK, 768), lambda h, info: (0, 0, 0))] * 4,
        scratch_shapes=[
            pltpu.VMEM((1024, 768), BF16),
            pltpu.VMEM((1024, 128), F32),
            pltpu.VMEM((1024, 128), F32),
            pltpu.VMEM((128, 1024), BF16),
        ],
    )
    return pl.pallas_call(
        attention_kernel,
        out_shape=[jax.ShapeDtypeStruct((2, TOK, 768), BF16)] * 4,
        grid_spec=grid_spec,
        compiler_params=params(),
        cost_estimate=pl.CostEstimate(
            flops=14 * 10**9,
            bytes_accessed=8 * 1024 * 1024,
            transcendentals=4 * 10 * 256 * 256,
        ),
    )(info, packed, packed, packed, mine, theirs, o_own, o_sib)


def merge_kernel(info, *refs):
    *near, far, queries, keys, values = refs
    here, core = info[0], info[3]
    for step in range(4):
        chip = lax.rem(here - step + 4, 4)
        mine, theirs = near[step][0], far[step]
        spot = chip * 1024 + core * 512
        queries[:, pl.ds(pl.multiple_of(spot, 512), 512)] = mine[:, :512]
        spot = chip * 1024 + (1 - core) * 512
        queries[:, pl.ds(pl.multiple_of(spot, 512), 512)] = theirs[:, :512]
        both = mine[:, 512:].astype(F32) + theirs[:, 512:].astype(F32)
        spot = pl.ds(pl.multiple_of(chip * 128, 128), 128)
        keys[:, spot] = both[:, :128].astype(BF16)
        values[:, spot] = both[:, 128:].astype(BF16)


def merge(info, near, far):
    whole = pl.BlockSpec(memory_space=pltpu.VMEM)
    return pl.pallas_call(
        merge_kernel,
        out_shape=(
            jax.ShapeDtypeStruct((TOK, 4096), BF16),
            jax.ShapeDtypeStruct((TOK, 512), BF16),
            jax.ShapeDtypeStruct((TOK, 512), BF16),
        ),
        in_specs=[pl.BlockSpec(memory_space=pltpu.SMEM)] + [whole] * 5,
        out_specs=(whole, whole, whole),
        compiler_params=params(),
    )(info, *near, far)


def add(*terms):
    total = terms[0].astype(F32)
    for term in terms[1:]:
        total = total + term.astype(F32)
    return total


def per_device(queries, keys, values, attn_out, out_grad, out_weight, lengths):
    x, core, y, z = (lax.axis_index(name) for name in ("x", "core", "y", "z"))
    info = jnp.stack([x, y, z, core]).astype(jnp.int32)
    info = jnp.concatenate([info, lengths[0]])
    factor = 32768 ** (-0.5)

    def halves(value):
        left, right = value[:, :2560], value[:, 2560:]
        return jnp.where(core == 0, left, right), jnp.where(core == 0, right, left)

    weight_mine, weight_theirs = halves(out_weight)
    weight_pair = jnp.stack([weight_mine, swap(weight_theirs)])
    near = jnp.stack([weight_pair] + [shift(weight_pair, "y", r) for r in (1, 2, 3)])

    o_split = jnp.transpose(attn_out.reshape(TOK, 4, 1024), (1, 0, 2))
    grad_mine, grad_theirs = halves(out_grad[0])
    own = (grad_mine, swap(grad_theirs))
    weight = lax.all_gather(after(near, o_split, grad_mine), "z", axis=0, tiled=False)
    o_own = lax.all_to_all(o_split, "x", split_axis=0, concat_axis=0, tiled=True)
    o_own = o_own.reshape(512, 1024)

    packed = jnp.concatenate(
        [
            queries.reshape(TOK, 8, 512),
            jnp.repeat(keys[0], 2, axis=1),
            jnp.repeat(values[0], 2, axis=1),
        ],
        axis=2,
    )
    packed = jnp.transpose(packed, (1, 0, 2))

    prev0, prev1 = (shift(part, "x", 1) for part in own)
    succ0, succ1 = (shift(part, "x", -1) for part in own)
    prev0, succ1, packed, o_own = lax.optimization_barrier((prev0, succ1, packed, o_own))
    packed = lax.all_to_all(packed, ("x", "core"), split_axis=0, concat_axis=0, tiled=True)
    packed = packed.reshape(1024, 768)
    o_sib = swap(o_own)
    far0, far1 = shift(prev0, "x", 1), shift(succ1, "x", -1)
    parts = (*own, prev0, prev1, succ0, succ1, far0, far1)
    term, rows = weight_product(info, parts, turn(o_own, o_sib), factor)

    summed = lax.psum_scatter(term, "z", scatter_dimension=0, tiled=True)[0]

    theirs = swap(project(info, rows, weight, 1, BF16))
    mine = project(info, rows, weight, 0, F32)
    grads = attention(info, packed, mine, theirs, o_own, o_sib)

    back = [grads[0]] + [shift(grads[r], "x", r) for r in (1, 2, 3)]
    grad_queries, grad_keys, grad_values = merge(
        info, back, swap(jnp.stack([part[1] for part in back]))
    )

    summed = after(summed, *back[1:])
    summed = [summed[0]] + [shift(summed[r], "y", r) for r in (1, 2, 3)]
    grad_queries = grad_queries.reshape(1, TOK, 32, 128)
    *summed, grad_queries, grad_keys, grad_values = lax.optimization_barrier(
        (*summed, grad_queries, grad_keys, grad_values)
    )
    summed = add(*summed)
    keep = jnp.where(core == 0, summed[0], summed[1])
    give = jnp.where(core == 0, summed[1], summed[0])
    come = swap(give)
    grad_out_weight = jnp.concatenate(
        [jnp.where(core == 0, keep, come), jnp.where(core == 0, come, keep)], axis=-1
    ).astype(F32)

    return (
        grad_queries,
        grad_keys.reshape(1, TOK, 4, 128),
        grad_values.reshape(1, TOK, 4, 128),
        grad_out_weight,
    )


def solution(mesh):
    mesh = Mesh(mesh.devices.reshape(4, 2, 4, 8), ("x", "core", "y", "z"))
    pack, token = ("y", "z"), ("x", "core")
    placed = (
        P(pack, token, None, None),
        P(pack, token, None, None),
        P(pack, token, None, None),
        P(pack, token, None, None),
        P(pack, token, None),
        P(token + pack, None),
        P(pack, None),
    )
    return jax.shard_map(
        per_device,
        mesh=mesh,
        in_specs=placed,
        out_specs=(
            P(pack, token, None, None),
            P(pack, token, None, None),
            P(pack, token, None, None),
            P(token + pack, None),
        ),
        check_vma=False,
    )
```

```python
import functools
import math

import jax
import jax.numpy as jnp
from jax import lax
from jax.experimental import pallas as pl
from jax.experimental.pallas import tpu as pltpu
from jax.sharding import Mesh
from jax.sharding import PartitionSpec as P

TOK = 128
QB = 256
COLS = 512
SPLIT = 4
PCOLS = 1280
F32 = jnp.float32
BF16 = jnp.bfloat16
VMEM = 56 * 1024 * 1024


def params():
    return pltpu.CompilerParams(vmem_limit_bytes=VMEM)


def shift(value, axis, by):
    size = lax.axis_size(axis)
    return lax.ppermute(value, axis, [(i, (i + by) % size) for i in range(size)])


def after(value, *others):
    return lax.optimization_barrier((value, *others))[0]


def swap(value):
    return lax.ppermute(value, "core", [(0, 1), (1, 0)])


def turn_kernel(o_own, o_sib, turned):
    turned[:, :512] = o_own[...].T
    turned[:, 512:] = o_sib[...].T


def turn(o_own, o_sib):
    whole = pl.BlockSpec(memory_space=pltpu.VMEM)
    return pl.pallas_call(
        turn_kernel,
        out_shape=jax.ShapeDtypeStruct((1024, 1024), BF16),
        in_specs=[whole, whole],
        out_specs=whole,
        compiler_params=params(),
    )(o_own, o_sib)


def weight_kernel(factor, info, *refs):
    *parts, turned, z_first, y0, y1, y2, y3, rows, product = refs
    here, y, z = info[0], info[1], info[2]
    step = pl.program_id(0)
    for place, (chip, rc) in enumerate((hop, rc) for hop in (0, 3, 1, 2) for rc in range(2)):
        spot = rc * 512 + lax.rem(here + chip, 4) * TOK
        rows[pl.ds(pl.multiple_of(spot, TOK), TOK), :] = parts[place][...]

    def term(part):
        block = turned[part * 256 : part * 256 + 256, :]
        value = jnp.dot(block, rows[...], preferred_element_type=F32)
        return (value * factor).astype(BF16)

    @pl.when(step < SPLIT)
    def _():
        for part in range(4):
            value = term(part)
            for at in range(16):
                f = part % 2 * 16 + at
                ry = lax.rem(f // 8 - y + 4, 4)
                z_first[f % 8, ry, part // 2] = value[at * 16 : at * 16 + 16, :]

    @pl.when(step >= SPLIT)
    def _():
        for part in range(4):
            product[part * 256 : part * 256 + 256, :] = term(part)
        for r, out in enumerate((y0, y1, y2, y3)):
            for at in range(8):
                f = lax.rem(y + r, 4) * 8 + lax.rem(z + at, 8)
                for kk in range(2):
                    row = pl.multiple_of(kk * 512 + f * 16, 16)
                    out[at, kk] = product[pl.ds(row, 16), :]


def weight_product(info, parts, turned, factor):
    grid_spec = pltpu.PrefetchScalarGridSpec(
        num_scalar_prefetch=1,
        grid=(2560 // COLS,),
        in_specs=[pl.BlockSpec((p.shape[0], COLS), lambda n, info: (0, n)) for p in parts]
        + [pl.BlockSpec((1024, 1024), lambda n, info: (0, 0))],
        out_specs=(
            pl.BlockSpec(
                (8, 4, 2, 16, COLS), lambda n, info: (0, 0, 0, 0, jnp.minimum(n, SPLIT - 1))
            ),
            *[pl.BlockSpec((8, 2, 16, COLS), lambda n, info: (0, 0, 0, 0)) for _ in range(4)],
            pl.BlockSpec((1024, COLS), lambda n, info: (0, n)),
        ),
        scratch_shapes=[pltpu.VMEM((1024, COLS), BF16)],
    )
    return pl.pallas_call(
        functools.partial(weight_kernel, factor),
        out_shape=(
            jax.ShapeDtypeStruct((8, 4, 2, 16, SPLIT * COLS), BF16),
            *[jax.ShapeDtypeStruct((8, 2, 16, COLS), BF16) for _ in range(4)],
            jax.ShapeDtypeStruct((1024, 2560), BF16),
        ),
        grid_spec=grid_spec,
        compiler_params=params(),
        cost_estimate=pl.CostEstimate(
            flops=1024 * 1024, bytes_accessed=1024 * 1024, transcendentals=0
        ),
    )(info, *parts, turned)


def project_kernel(info, rows, block, out, total):
    core = info[3]
    step = pl.program_id(0)
    product = lax.dot_general(
        rows[...],
        block[...].reshape(512, PCOLS),
        (((1,), (1,)), ((), ())),
        preferred_element_type=F32,
    )

    @pl.when(step == 0)
    def _():
        total[...] = product

    @pl.when(step > 0)
    def _():
        total[...] += product

    @pl.when(step == pl.num_programs(0) - 1)
    def _():
        for rc in range(2):
            for chip in range(4):
                at = rc * 512 + chip * TOK
                spot = chip * 256 + (core if rc == 0 else 1 - core) * TOK
                spot = pl.ds(pl.multiple_of(spot, TOK), TOK)
                out[spot, :] = total[at : at + TOK, :].astype(out.dtype)


def project(info, rows, weight, rc, dtype):
    grid_spec = pltpu.PrefetchScalarGridSpec(
        num_scalar_prefetch=1,
        grid=(2560 // PCOLS,),
        in_specs=[
            pl.BlockSpec((1024, PCOLS), lambda n, info: (0, n)),
            pl.BlockSpec((32, None, 16, PCOLS), lambda n, info: (0, rc, 0, n)),
        ],
        out_specs=pl.BlockSpec((1024, 512), lambda n, info: (0, 0)),
        scratch_shapes=[pltpu.VMEM((1024, 512), F32)],
    )
    return pl.pallas_call(
        project_kernel,
        out_shape=jax.ShapeDtypeStruct((1024, 512), dtype),
        grid_spec=grid_spec,
        compiler_params=params(),
        cost_estimate=pl.CostEstimate(
            flops=1024 * 1024, bytes_accessed=1024 * 1024, transcendentals=0
        ),
    )(info, rows, weight)


def attention_kernel(info, query, key, value, mine, theirs, o_own, o_sib, *outs):
    *outs, out, key_acc, value_acc, turned = outs
    head = pl.program_id(0)
    here, core = info[0], info[3]
    ends = (info[4], info[4] + info[5], info[4] + info[5] + info[6])
    scale = 128 ** (-0.5)

    @pl.when(head == 0)
    def _():
        key_acc[...] = jnp.zeros_like(key_acc)
        value_acc[...] = jnp.zeros_like(value_acc)
        turned[...] = key[...].T

    for block in range(4):
        at = block * QB
        begin = max(0, at - 512)
        span = at + QB - begin
        rows = slice(at, at + QB)
        cols = slice(begin, at + QB)
        q = query[rows, :]
        k = key[cols, :]
        v = value[cols, :]
        grad = (mine[rows, :].astype(F32) + theirs[rows, :].astype(F32)).astype(BF16)
        near = o_own[block * TOK : block * TOK + TOK, :].astype(F32)
        other = o_sib[block * TOK : block * TOK + TOK, :].astype(F32)
        saved = jnp.concatenate(
            [jnp.where(core == 0, near, other), jnp.where(core == 0, other, near)], axis=0
        )
        delta = jnp.sum((grad.astype(F32) * saved).T, axis=0, keepdims=True)
        i = at + lax.broadcasted_iota(jnp.int32, (1, QB), 1)
        start = jnp.zeros_like(i)
        for end in ends:
            start = jnp.where(i >= end, end, start)
        j = begin + lax.broadcasted_iota(jnp.int32, (span, QB), 0)
        scores = lax.dot_general(k, q, (((1,), (1,)), ((), ())), preferred_element_type=F32)
        scores = jnp.where((j <= i) & (j >= start), scores, -1e30)
        top = jnp.max(scores, axis=0, keepdims=True)
        raised = jnp.exp2((scores - top) * (scale * math.log2(math.e)))
        soft = raised * (1.0 / jnp.sum(raised, axis=0, keepdims=True))
        value_acc[cols, :] += jnp.dot(soft.astype(BF16), grad, preferred_element_type=F32)
        grad_soft = lax.dot_general(v, grad, (((1,), (1,)), ((), ())), preferred_element_type=F32)
        grad_scores = (soft * (grad_soft - delta)).astype(BF16)
        key_acc[cols, :] += jnp.dot(grad_scores, q, preferred_element_type=F32)
        grad_query = jnp.dot(turned[:, cols], grad_scores, preferred_element_type=F32).T * scale
        out[rows, pl.ds(pl.multiple_of(head * 128, 128), 128)] = grad_query.astype(BF16)

    @pl.when(head == 3)
    def _():
        out[:, 512:640] = (key_acc[...] * scale).astype(BF16)
        out[:, 640:768] = value_acc[...].astype(BF16)
        for step in range(4):
            for rc in range(2):
                row = lax.rem(here + step, 4) * 256 + (core if rc == 0 else 1 - core) * TOK
                outs[step][rc] = out[pl.ds(pl.multiple_of(row, TOK), TOK), :]


def attention(info, packed, mine, theirs, o_own, o_sib):
    grid_spec = pltpu.PrefetchScalarGridSpec(
        num_scalar_prefetch=1,
        grid=(4,),
        in_specs=[
            pl.BlockSpec((1024, 128), lambda h, info: (0, h)),
            pl.BlockSpec((1024, 128), lambda h, info: (0, 4)),
            pl.BlockSpec((1024, 128), lambda h, info: (0, 5)),
            pl.BlockSpec((1024, 128), lambda h, info: (0, h)),
            pl.BlockSpec((1024, 128), lambda h, info: (0, h)),
            pl.BlockSpec((512, 128), lambda h, info: (0, info[3] * 4 + h)),
            pl.BlockSpec((512, 128), lambda h, info: (0, info[3] * 4 + h)),
        ],
        out_specs=[pl.BlockSpec((2, TOK, 768), lambda h, info: (0, 0, 0))] * 4,
        scratch_shapes=[
            pltpu.VMEM((1024, 768), BF16),
            pltpu.VMEM((1024, 128), F32),
            pltpu.VMEM((1024, 128), F32),
            pltpu.VMEM((128, 1024), BF16),
        ],
    )
    return pl.pallas_call(
        attention_kernel,
        out_shape=[jax.ShapeDtypeStruct((2, TOK, 768), BF16)] * 4,
        grid_spec=grid_spec,
        compiler_params=params(),
        cost_estimate=pl.CostEstimate(
            flops=14 * 10**9,
            bytes_accessed=8 * 1024 * 1024,
            transcendentals=4 * 10 * 256 * 256,
        ),
    )(info, packed, packed, packed, mine, theirs, o_own, o_sib)


def merge_kernel(info, *refs):
    *near, far, queries, keys, values = refs
    here, core = info[0], info[3]
    for step in range(4):
        chip = lax.rem(here - step + 4, 4)
        mine, theirs = near[step][0], far[step]
        spot = chip * 1024 + core * 512
        queries[:, pl.ds(pl.multiple_of(spot, 512), 512)] = mine[:, :512]
        spot = chip * 1024 + (1 - core) * 512
        queries[:, pl.ds(pl.multiple_of(spot, 512), 512)] = theirs[:, :512]
        both = mine[:, 512:].astype(F32) + theirs[:, 512:].astype(F32)
        spot = pl.ds(pl.multiple_of(chip * 128, 128), 128)
        keys[:, spot] = both[:, :128].astype(BF16)
        values[:, spot] = both[:, 128:].astype(BF16)


def merge(info, near, far):
    whole = pl.BlockSpec(memory_space=pltpu.VMEM)
    return pl.pallas_call(
        merge_kernel,
        out_shape=(
            jax.ShapeDtypeStruct((TOK, 4096), BF16),
            jax.ShapeDtypeStruct((TOK, 512), BF16),
            jax.ShapeDtypeStruct((TOK, 512), BF16),
        ),
        in_specs=[pl.BlockSpec(memory_space=pltpu.SMEM)] + [whole] * 5,
        out_specs=(whole, whole, whole),
        compiler_params=params(),
    )(info, *near, far)


def add(*terms):
    total = terms[0].astype(F32)
    for term in terms[1:]:
        total = total + term.astype(F32)
    return total


def per_device(queries, keys, values, attn_out, out_grad, out_weight, lengths):
    x, core, y, z = (lax.axis_index(name) for name in ("x", "core", "y", "z"))
    info = jnp.stack([x, y, z, core]).astype(jnp.int32)
    info = jnp.concatenate([info, lengths[0]])
    factor = 32768 ** (-0.5)

    def halves(value):
        left, right = value[:, :2560], value[:, 2560:]
        return jnp.where(core == 0, left, right), jnp.where(core == 0, right, left)

    weight_mine, weight_theirs = halves(out_weight)
    weight_pair = jnp.stack([weight_mine, swap(weight_theirs)])
    weight = lax.all_gather(weight_pair, ("y", "z"), axis=0, tiled=False)

    o_split = jnp.transpose(attn_out.reshape(TOK, 4, 1024), (1, 0, 2))
    grad_mine, grad_theirs = halves(out_grad[0])
    own = (grad_mine, swap(grad_theirs))
    o_own = lax.all_to_all(o_split, "x", split_axis=0, concat_axis=0, tiled=True)
    o_own = o_own.reshape(512, 1024)

    packed = jnp.concatenate(
        [
            queries.reshape(TOK, 8, 512),
            jnp.repeat(keys[0], 2, axis=1),
            jnp.repeat(values[0], 2, axis=1),
        ],
        axis=2,
    )
    packed = jnp.transpose(packed, (1, 0, 2))

    prev0, prev1 = (shift(part, "x", 1) for part in own)
    succ0, succ1 = (shift(part, "x", -1) for part in own)
    prev0, succ1, packed, o_own = lax.optimization_barrier((prev0, succ1, packed, o_own))
    packed = lax.all_to_all(packed, ("x", "core"), split_axis=0, concat_axis=0, tiled=True)
    packed = packed.reshape(1024, 768)
    o_sib = swap(o_own)
    far0, far1 = shift(prev0, "x", 1), shift(succ1, "x", -1)
    parts = (*own, prev0, prev1, succ0, succ1, far0, far1)
    z_first, *y_first, rows = weight_product(info, parts, turn(o_own, o_sib), factor)

    z_first = lax.psum_scatter(z_first, "z", scatter_dimension=0, tiled=True)[0]
    y_first = [y_first[0]] + [shift(y_first[r], "y", r) for r in (1, 2, 3)]

    theirs = swap(project(info, rows, weight, 1, BF16))
    mine = project(info, rows, weight, 0, F32)
    grads = attention(info, packed, mine, theirs, o_own, o_sib)
    *y_first, g0, g1, g2, g3 = lax.optimization_barrier((*y_first, *grads))

    back = [g0, shift(g1, "x", 1), shift(g2, "x", 2), shift(g3, "x", 3)]
    grad_queries, grad_keys, grad_values = merge(
        info, back, swap(jnp.stack([part[1] for part in back]))
    )

    y_first = add(*y_first).astype(BF16)
    z_first, y_first = after(z_first, *back[1:]), after(y_first, *back[1:])
    z_first = [z_first[0]] + [shift(z_first[r], "y", r) for r in (1, 2, 3)]
    y_first = [y_first[0]] + [shift(y_first[r], "z", r) for r in range(1, 8)]
    grad_queries = grad_queries.reshape(1, TOK, 32, 128)
    *z_first, grad_queries, grad_keys, grad_values = lax.optimization_barrier(
        (*z_first, grad_queries, grad_keys, grad_values)
    )
    summed = jnp.concatenate([add(*z_first), add(*y_first)], axis=-1)
    keep = jnp.where(core == 0, summed[0], summed[1])
    give = jnp.where(core == 0, summed[1], summed[0])
    come = swap(give)
    grad_out_weight = jnp.concatenate(
        [jnp.where(core == 0, keep, come), jnp.where(core == 0, come, keep)], axis=-1
    ).astype(F32)

    return (
        grad_queries,
        grad_keys.reshape(1, TOK, 4, 128),
        grad_values.reshape(1, TOK, 4, 128),
        grad_out_weight,
    )


def solution(mesh):
    mesh = Mesh(mesh.devices.reshape(4, 2, 4, 8), ("x", "core", "y", "z"))
    pack, token = ("y", "z"), ("x", "core")
    placed = (
        P(pack, token, None, None),
        P(pack, token, None, None),
        P(pack, token, None, None),
        P(pack, token, None, None),
        P(pack, token, None),
        P(token + pack, None),
        P(pack, None),
    )
    return jax.shard_map(
        per_device,
        mesh=mesh,
        in_specs=placed,
        out_specs=(
            P(pack, token, None, None),
            P(pack, token, None, None),
            P(pack, token, None, None),
            P(token + pack, None),
        ),
        check_vma=False,
    )
```

```python
import functools
import math

import jax
import jax.numpy as jnp
from jax import lax
from jax.experimental import pallas as pl
from jax.experimental.pallas import tpu as pltpu
from jax.sharding import Mesh
from jax.sharding import PartitionSpec as P

TOK = 128
QB = 256
COLS = 512
PCOLS = 1280
F32 = jnp.float32
BF16 = jnp.bfloat16
VMEM = 56 * 1024 * 1024


def params():
    return pltpu.CompilerParams(vmem_limit_bytes=VMEM)


def shift(value, axis, by):
    size = lax.axis_size(axis)
    return lax.ppermute(value, axis, [(i, (i + by) % size) for i in range(size)])


def after(value, *others):
    return lax.optimization_barrier((value, *others))[0]


def swap(value):
    return lax.ppermute(value, "core", [(0, 1), (1, 0)])


def turn_kernel(o_own, o_sib, turned):
    turned[:, :512] = o_own[...].T
    turned[:, 512:] = o_sib[...].T


def turn(o_own, o_sib):
    whole = pl.BlockSpec(memory_space=pltpu.VMEM)
    return pl.pallas_call(
        turn_kernel,
        out_shape=jax.ShapeDtypeStruct((1024, 1024), BF16),
        in_specs=[whole, whole],
        out_specs=whole,
        compiler_params=params(),
    )(o_own, o_sib)


def weight_kernel(factor, info, *refs):
    *parts, turned, term, rows = refs
    here, y = info[0], info[1]
    for place, (chip, rc) in enumerate((step, rc) for step in (0, 3, 1, 2) for rc in range(2)):
        spot = rc * 512 + lax.rem(here + chip, 4) * TOK
        rows[pl.ds(pl.multiple_of(spot, TOK), TOK), :] = parts[place][...]
    for part in range(4):
        product = jnp.dot(
            turned[part * 256 : part * 256 + 256, :], rows[...], preferred_element_type=F32
        )
        product = (product * factor).astype(BF16)
        for at in range(16):
            f = part % 2 * 16 + at
            ry = lax.rem(f // 8 - y + 4, 4)
            term[f % 8, ry, part // 2] = product[at * 16 : at * 16 + 16, :]


def weight_product(info, parts, turned, factor):
    grid_spec = pltpu.PrefetchScalarGridSpec(
        num_scalar_prefetch=1,
        grid=(2560 // COLS,),
        in_specs=[pl.BlockSpec((p.shape[0], COLS), lambda n, info: (0, n)) for p in parts]
        + [pl.BlockSpec((1024, 1024), lambda n, info: (0, 0))],
        out_specs=(
            pl.BlockSpec((8, 4, 2, 16, COLS), lambda n, info: (0, 0, 0, 0, n)),
            pl.BlockSpec((1024, COLS), lambda n, info: (0, n)),
        ),
    )
    return pl.pallas_call(
        functools.partial(weight_kernel, factor),
        out_shape=(
            jax.ShapeDtypeStruct((8, 4, 2, 16, 2560), BF16),
            jax.ShapeDtypeStruct((1024, 2560), BF16),
        ),
        grid_spec=grid_spec,
        compiler_params=params(),
        cost_estimate=pl.CostEstimate(
            flops=1024 * 1024, bytes_accessed=1024 * 1024, transcendentals=0
        ),
    )(info, *parts, turned)


def project_kernel(info, rows, block, out, total):
    core = info[3]
    step = pl.program_id(0)
    product = lax.dot_general(
        rows[...],
        block[...].reshape(512, PCOLS),
        (((1,), (1,)), ((), ())),
        preferred_element_type=F32,
    )

    @pl.when(step == 0)
    def _():
        total[...] = product

    @pl.when(step > 0)
    def _():
        total[...] += product

    @pl.when(step == pl.num_programs(0) - 1)
    def _():
        for rc in range(2):
            for chip in range(4):
                at = rc * 512 + chip * TOK
                spot = chip * 256 + (core if rc == 0 else 1 - core) * TOK
                spot = pl.ds(pl.multiple_of(spot, TOK), TOK)
                out[spot, :] = total[at : at + TOK, :].astype(out.dtype)


def project(info, rows, weight, rc, dtype):
    grid_spec = pltpu.PrefetchScalarGridSpec(
        num_scalar_prefetch=1,
        grid=(2560 // PCOLS,),
        in_specs=[
            pl.BlockSpec((1024, PCOLS), lambda n, info: (0, n)),
            pl.BlockSpec((32, None, 16, PCOLS), lambda n, info: (0, rc, 0, n)),
        ],
        out_specs=pl.BlockSpec((1024, 512), lambda n, info: (0, 0)),
        scratch_shapes=[pltpu.VMEM((1024, 512), F32)],
    )
    return pl.pallas_call(
        project_kernel,
        out_shape=jax.ShapeDtypeStruct((1024, 512), dtype),
        grid_spec=grid_spec,
        compiler_params=params(),
        cost_estimate=pl.CostEstimate(
            flops=1024 * 1024, bytes_accessed=1024 * 1024, transcendentals=0
        ),
    )(info, rows, weight)


def attention_kernel(info, query, key, value, mine, theirs, o_own, o_sib, *outs):
    *outs, out, key_acc, value_acc, turned = outs
    head = pl.program_id(0)
    here, core = info[0], info[3]
    ends = (info[4], info[4] + info[5], info[4] + info[5] + info[6])
    scale = 128 ** (-0.5)

    @pl.when(head == 0)
    def _():
        key_acc[...] = jnp.zeros_like(key_acc)
        value_acc[...] = jnp.zeros_like(value_acc)
        turned[...] = key[...].T

    for block in range(4):
        at = block * QB
        begin = max(0, at - 512)
        span = at + QB - begin
        rows = slice(at, at + QB)
        cols = slice(begin, at + QB)
        q = query[rows, :]
        k = key[cols, :]
        v = value[cols, :]
        grad = (mine[rows, :].astype(F32) + theirs[rows, :].astype(F32)).astype(BF16)
        near = o_own[block * TOK : block * TOK + TOK, :].astype(F32)
        other = o_sib[block * TOK : block * TOK + TOK, :].astype(F32)
        saved = jnp.concatenate(
            [jnp.where(core == 0, near, other), jnp.where(core == 0, other, near)], axis=0
        )
        delta = jnp.sum((grad.astype(F32) * saved).T, axis=0, keepdims=True)
        i = at + lax.broadcasted_iota(jnp.int32, (1, QB), 1)
        start = jnp.zeros_like(i)
        for end in ends:
            start = jnp.where(i >= end, end, start)
        j = begin + lax.broadcasted_iota(jnp.int32, (span, QB), 0)
        scores = lax.dot_general(k, q, (((1,), (1,)), ((), ())), preferred_element_type=F32)
        scores = jnp.where((j <= i) & (j >= start), scores, -1e30)
        top = jnp.max(scores, axis=0, keepdims=True)
        raised = jnp.exp2((scores - top) * (scale * math.log2(math.e)))
        soft = raised * (1.0 / jnp.sum(raised, axis=0, keepdims=True))
        value_acc[cols, :] += jnp.dot(soft.astype(BF16), grad, preferred_element_type=F32)
        grad_soft = lax.dot_general(v, grad, (((1,), (1,)), ((), ())), preferred_element_type=F32)
        grad_scores = (soft * (grad_soft - delta)).astype(BF16)
        key_acc[cols, :] += jnp.dot(grad_scores, q, preferred_element_type=F32)
        grad_query = jnp.dot(turned[:, cols], grad_scores, preferred_element_type=F32).T * scale
        out[rows, pl.ds(pl.multiple_of(head * 128, 128), 128)] = grad_query.astype(BF16)

    @pl.when(head == 3)
    def _():
        out[:, 512:640] = (key_acc[...] * scale).astype(BF16)
        out[:, 640:768] = value_acc[...].astype(BF16)
        for step in range(4):
            for rc in range(2):
                row = lax.rem(here + step, 4) * 256 + (core if rc == 0 else 1 - core) * TOK
                outs[step][rc] = out[pl.ds(pl.multiple_of(row, TOK), TOK), :]


def attention(info, packed, mine, theirs, o_own, o_sib):
    grid_spec = pltpu.PrefetchScalarGridSpec(
        num_scalar_prefetch=1,
        grid=(4,),
        in_specs=[
            pl.BlockSpec((1024, 128), lambda h, info: (0, h)),
            pl.BlockSpec((1024, 128), lambda h, info: (0, 4)),
            pl.BlockSpec((1024, 128), lambda h, info: (0, 5)),
            pl.BlockSpec((1024, 128), lambda h, info: (0, h)),
            pl.BlockSpec((1024, 128), lambda h, info: (0, h)),
            pl.BlockSpec((512, 128), lambda h, info: (0, info[3] * 4 + h)),
            pl.BlockSpec((512, 128), lambda h, info: (0, info[3] * 4 + h)),
        ],
        out_specs=[pl.BlockSpec((2, TOK, 768), lambda h, info: (0, 0, 0))] * 4,
        scratch_shapes=[
            pltpu.VMEM((1024, 768), BF16),
            pltpu.VMEM((1024, 128), F32),
            pltpu.VMEM((1024, 128), F32),
            pltpu.VMEM((128, 1024), BF16),
        ],
    )
    return pl.pallas_call(
        attention_kernel,
        out_shape=[jax.ShapeDtypeStruct((2, TOK, 768), BF16)] * 4,
        grid_spec=grid_spec,
        compiler_params=params(),
        cost_estimate=pl.CostEstimate(
            flops=14 * 10**9,
            bytes_accessed=8 * 1024 * 1024,
            transcendentals=4 * 10 * 256 * 256,
        ),
    )(info, packed, packed, packed, mine, theirs, o_own, o_sib)


def merge_kernel(info, *refs):
    *near, far, queries, keys, values = refs
    here, core = info[0], info[3]
    for step in range(4):
        chip = lax.rem(here - step + 4, 4)
        mine, theirs = near[step][0], far[step]
        spot = chip * 1024 + core * 512
        queries[:, pl.ds(pl.multiple_of(spot, 512), 512)] = mine[:, :512]
        spot = chip * 1024 + (1 - core) * 512
        queries[:, pl.ds(pl.multiple_of(spot, 512), 512)] = theirs[:, :512]
        both = mine[:, 512:].astype(F32) + theirs[:, 512:].astype(F32)
        spot = pl.ds(pl.multiple_of(chip * 128, 128), 128)
        keys[:, spot] = both[:, :128].astype(BF16)
        values[:, spot] = both[:, 128:].astype(BF16)


def merge(info, near, far):
    whole = pl.BlockSpec(memory_space=pltpu.VMEM)
    return pl.pallas_call(
        merge_kernel,
        out_shape=(
            jax.ShapeDtypeStruct((TOK, 4096), BF16),
            jax.ShapeDtypeStruct((TOK, 512), BF16),
            jax.ShapeDtypeStruct((TOK, 512), BF16),
        ),
        in_specs=[pl.BlockSpec(memory_space=pltpu.SMEM)] + [whole] * 5,
        out_specs=(whole, whole, whole),
        compiler_params=params(),
    )(info, *near, far)


def add(*terms):
    total = terms[0].astype(F32)
    for term in terms[1:]:
        total = total + term.astype(F32)
    return total


def per_device(queries, keys, values, attn_out, out_grad, out_weight, lengths):
    x, core, y, z = (lax.axis_index(name) for name in ("x", "core", "y", "z"))
    info = jnp.stack([x, y, z, core]).astype(jnp.int32)
    info = jnp.concatenate([info, lengths[0]])
    factor = 32768 ** (-0.5)

    def halves(value):
        left, right = value[:, :2560], value[:, 2560:]
        return jnp.where(core == 0, left, right), jnp.where(core == 0, right, left)

    weight_mine, weight_theirs = halves(out_weight)
    weight_pair = jnp.stack([weight_mine, swap(weight_theirs)])
    weight = lax.all_gather(weight_pair, ("y", "z"), axis=0, tiled=False)

    o_split = jnp.transpose(attn_out.reshape(TOK, 4, 1024), (1, 0, 2))
    grad_mine, grad_theirs = halves(out_grad[0])
    own = (grad_mine, swap(grad_theirs))
    o_own = lax.all_to_all(o_split, "x", split_axis=0, concat_axis=0, tiled=True)
    o_own = o_own.reshape(512, 1024)

    packed = jnp.concatenate(
        [
            queries.reshape(TOK, 8, 512),
            jnp.repeat(keys[0], 2, axis=1),
            jnp.repeat(values[0], 2, axis=1),
        ],
        axis=2,
    )
    packed = jnp.transpose(packed, (1, 0, 2))

    prev0, prev1 = (shift(part, "x", 1) for part in own)
    succ0, succ1 = (shift(part, "x", -1) for part in own)
    prev0, succ1, packed, o_own = lax.optimization_barrier((prev0, succ1, packed, o_own))
    packed = lax.all_to_all(packed, ("x", "core"), split_axis=0, concat_axis=0, tiled=True)
    packed = packed.reshape(1024, 768)
    o_sib = swap(o_own)
    far0, far1 = shift(prev0, "x", 1), shift(succ1, "x", -1)
    parts = (*own, prev0, prev1, succ0, succ1, far0, far1)
    term, rows = weight_product(info, parts, turn(o_own, o_sib), factor)

    summed = lax.psum_scatter(term, "z", scatter_dimension=0, tiled=True)[0]

    theirs = swap(project(info, rows, weight, 1, BF16))
    mine = project(info, rows, weight, 0, F32)
    grads = attention(info, packed, mine, theirs, o_own, o_sib)

    back = [grads[0]] + [shift(grads[r], "x", r) for r in (1, 2, 3)]
    grad_queries, grad_keys, grad_values = merge(
        info, back, swap(jnp.stack([part[1] for part in back]))
    )

    summed = after(summed, *back[1:])
    summed = [summed[0]] + [shift(summed[r], "y", r) for r in (1, 2, 3)]
    grad_queries = grad_queries.reshape(1, TOK, 32, 128)
    *summed, grad_queries, grad_keys, grad_values = lax.optimization_barrier(
        (*summed, grad_queries, grad_keys, grad_values)
    )
    summed = add(*summed)
    keep = jnp.where(core == 0, summed[0], summed[1])
    give = jnp.where(core == 0, summed[1], summed[0])
    come = swap(give)
    grad_out_weight = jnp.concatenate(
        [jnp.where(core == 0, keep, come), jnp.where(core == 0, come, keep)], axis=-1
    ).astype(F32)

    return (
        grad_queries,
        grad_keys.reshape(1, TOK, 4, 128),
        grad_values.reshape(1, TOK, 4, 128),
        grad_out_weight,
    )


def solution(mesh):
    mesh = Mesh(mesh.devices.reshape(4, 2, 4, 8), ("x", "core", "y", "z"))
    pack, token = ("y", "z"), ("x", "core")
    placed = (
        P(pack, token, None, None),
        P(pack, token, None, None),
        P(pack, token, None, None),
        P(pack, token, None, None),
        P(pack, token, None),
        P(token + pack, None),
        P(pack, None),
    )
    return jax.shard_map(
        per_device,
        mesh=mesh,
        in_specs=placed,
        out_specs=(
            P(pack, token, None, None),
            P(pack, token, None, None),
            P(pack, token, None, None),
            P(token + pack, None),
        ),
        check_vma=False,
    )
```

```python
import functools
import math

import jax
import jax.numpy as jnp
from jax import lax
from jax.experimental import pallas as pl
from jax.experimental.pallas import tpu as pltpu
from jax.sharding import Mesh
from jax.sharding import PartitionSpec as P

TOK = 128
QB = 256
COLS = 512
PCOLS = 1280
F32 = jnp.float32
BF16 = jnp.bfloat16
VMEM = 56 * 1024 * 1024


def params():
    return pltpu.CompilerParams(vmem_limit_bytes=VMEM)


def shift(value, axis, by):
    size = lax.axis_size(axis)
    return lax.ppermute(value, axis, [(i, (i + by) % size) for i in range(size)])


def after(value, *others):
    return lax.optimization_barrier((value, *others))[0]


def swap(value):
    return lax.ppermute(value, "core", [(0, 1), (1, 0)])


def turn_kernel(o_own, o_sib, turned):
    turned[:, :512] = o_own[...].T
    turned[:, 512:] = o_sib[...].T


def turn(o_own, o_sib):
    whole = pl.BlockSpec(memory_space=pltpu.VMEM)
    return pl.pallas_call(
        turn_kernel,
        out_shape=jax.ShapeDtypeStruct((1024, 1024), BF16),
        in_specs=[whole, whole],
        out_specs=whole,
        compiler_params=params(),
    )(o_own, o_sib)


def weight_kernel(factor, info, *refs):
    *parts, turned, term, rows = refs
    here, y = info[0], info[1]
    for place, (chip, rc) in enumerate((step, rc) for step in (0, 3, 1, 2) for rc in range(2)):
        spot = rc * 512 + lax.rem(here + chip, 4) * TOK
        rows[pl.ds(pl.multiple_of(spot, TOK), TOK), :] = parts[place][...]
    for part in range(4):
        product = jnp.dot(
            turned[part * 256 : part * 256 + 256, :], rows[...], preferred_element_type=F32
        )
        product = (product * factor).astype(BF16)
        for at in range(16):
            f = part % 2 * 16 + at
            ry = lax.rem(f // 8 - y + 4, 4)
            term[f % 8, ry, part // 2] = product[at * 16 : at * 16 + 16, :]


def weight_product(info, parts, turned, factor):
    grid_spec = pltpu.PrefetchScalarGridSpec(
        num_scalar_prefetch=1,
        grid=(2560 // COLS,),
        in_specs=[pl.BlockSpec((p.shape[0], COLS), lambda n, info: (0, n)) for p in parts]
        + [pl.BlockSpec((1024, 1024), lambda n, info: (0, 0))],
        out_specs=(
            pl.BlockSpec((8, 4, 2, 16, COLS), lambda n, info: (0, 0, 0, 0, n)),
            pl.BlockSpec((1024, COLS), lambda n, info: (0, n)),
        ),
    )
    return pl.pallas_call(
        functools.partial(weight_kernel, factor),
        out_shape=(
            jax.ShapeDtypeStruct((8, 4, 2, 16, 2560), BF16),
            jax.ShapeDtypeStruct((1024, 2560), BF16),
        ),
        grid_spec=grid_spec,
        compiler_params=params(),
        cost_estimate=pl.CostEstimate(
            flops=1024 * 1024, bytes_accessed=1024 * 1024, transcendentals=0
        ),
    )(info, *parts, turned)


def project_kernel(info, rows, block, out, weight, total):
    y, core = info[1], info[3]
    step = pl.program_id(0)
    for r in range(4):
        for z in range(8):
            row = (lax.rem(y - r + 4, 4) * 8 + z) * 16
            weight[pl.ds(pl.multiple_of(row, 16), 16), :] = block[z, r]
    product = lax.dot_general(
        rows[...], weight[...], (((1,), (1,)), ((), ())), preferred_element_type=F32
    )

    @pl.when(step == 0)
    def _():
        total[...] = product

    @pl.when(step > 0)
    def _():
        total[...] += product

    @pl.when(step == pl.num_programs(0) - 1)
    def _():
        for rc in range(2):
            for chip in range(4):
                at = rc * 512 + chip * TOK
                spot = chip * 256 + (core if rc == 0 else 1 - core) * TOK
                spot = pl.ds(pl.multiple_of(spot, TOK), TOK)
                out[spot, :] = total[at : at + TOK, :].astype(out.dtype)


def project(info, rows, weight, rc, dtype):
    grid_spec = pltpu.PrefetchScalarGridSpec(
        num_scalar_prefetch=1,
        grid=(2560 // PCOLS,),
        in_specs=[
            pl.BlockSpec((1024, PCOLS), lambda n, info: (0, n)),
            pl.BlockSpec((8, 4, None, 16, PCOLS), lambda n, info: (0, 0, rc, 0, n)),
        ],
        out_specs=pl.BlockSpec((1024, 512), lambda n, info: (0, 0)),
        scratch_shapes=[pltpu.VMEM((512, PCOLS), BF16), pltpu.VMEM((1024, 512), F32)],
    )
    return pl.pallas_call(
        project_kernel,
        out_shape=jax.ShapeDtypeStruct((1024, 512), dtype),
        grid_spec=grid_spec,
        compiler_params=params(),
        cost_estimate=pl.CostEstimate(
            flops=1024 * 1024, bytes_accessed=1024 * 1024, transcendentals=0
        ),
    )(info, rows, weight)


def attention_kernel(info, query, key, value, mine, theirs, o_own, o_sib, *outs):
    *outs, out, key_acc, value_acc, turned = outs
    head = pl.program_id(0)
    here, core = info[0], info[3]
    ends = (info[4], info[4] + info[5], info[4] + info[5] + info[6])
    scale = 128 ** (-0.5)

    @pl.when(head == 0)
    def _():
        key_acc[...] = jnp.zeros_like(key_acc)
        value_acc[...] = jnp.zeros_like(value_acc)
        turned[...] = key[...].T

    for block in range(4):
        at = block * QB
        begin = max(0, at - 512)
        span = at + QB - begin
        rows = slice(at, at + QB)
        cols = slice(begin, at + QB)
        q = query[rows, :]
        k = key[cols, :]
        v = value[cols, :]
        grad = (mine[rows, :].astype(F32) + theirs[rows, :].astype(F32)).astype(BF16)
        near = o_own[block * TOK : block * TOK + TOK, :].astype(F32)
        other = o_sib[block * TOK : block * TOK + TOK, :].astype(F32)
        saved = jnp.concatenate(
            [jnp.where(core == 0, near, other), jnp.where(core == 0, other, near)], axis=0
        )
        delta = jnp.sum((grad.astype(F32) * saved).T, axis=0, keepdims=True)
        i = at + lax.broadcasted_iota(jnp.int32, (1, QB), 1)
        start = jnp.zeros_like(i)
        for end in ends:
            start = jnp.where(i >= end, end, start)
        j = begin + lax.broadcasted_iota(jnp.int32, (span, QB), 0)
        scores = lax.dot_general(k, q, (((1,), (1,)), ((), ())), preferred_element_type=F32)
        scores = jnp.where((j <= i) & (j >= start), scores, -1e30)
        top = jnp.max(scores, axis=0, keepdims=True)
        raised = jnp.exp2((scores - top) * (scale * math.log2(math.e)))
        soft = raised * (1.0 / jnp.sum(raised, axis=0, keepdims=True))
        value_acc[cols, :] += jnp.dot(soft.astype(BF16), grad, preferred_element_type=F32)
        grad_soft = lax.dot_general(v, grad, (((1,), (1,)), ((), ())), preferred_element_type=F32)
        grad_scores = (soft * (grad_soft - delta)).astype(BF16)
        key_acc[cols, :] += jnp.dot(grad_scores, q, preferred_element_type=F32)
        grad_query = jnp.dot(turned[:, cols], grad_scores, preferred_element_type=F32).T * scale
        out[rows, pl.ds(pl.multiple_of(head * 128, 128), 128)] = grad_query.astype(BF16)

    @pl.when(head == 3)
    def _():
        out[:, 512:640] = (key_acc[...] * scale).astype(BF16)
        out[:, 640:768] = value_acc[...].astype(BF16)
        for step in range(4):
            for rc in range(2):
                row = lax.rem(here + step, 4) * 256 + (core if rc == 0 else 1 - core) * TOK
                outs[step][rc] = out[pl.ds(pl.multiple_of(row, TOK), TOK), :]


def attention(info, packed, mine, theirs, o_own, o_sib):
    grid_spec = pltpu.PrefetchScalarGridSpec(
        num_scalar_prefetch=1,
        grid=(4,),
        in_specs=[
            pl.BlockSpec((1024, 128), lambda h, info: (0, h)),
            pl.BlockSpec((1024, 128), lambda h, info: (0, 4)),
            pl.BlockSpec((1024, 128), lambda h, info: (0, 5)),
            pl.BlockSpec((1024, 128), lambda h, info: (0, h)),
            pl.BlockSpec((1024, 128), lambda h, info: (0, h)),
            pl.BlockSpec((512, 128), lambda h, info: (0, info[3] * 4 + h)),
            pl.BlockSpec((512, 128), lambda h, info: (0, info[3] * 4 + h)),
        ],
        out_specs=[pl.BlockSpec((2, TOK, 768), lambda h, info: (0, 0, 0))] * 4,
        scratch_shapes=[
            pltpu.VMEM((1024, 768), BF16),
            pltpu.VMEM((1024, 128), F32),
            pltpu.VMEM((1024, 128), F32),
            pltpu.VMEM((128, 1024), BF16),
        ],
    )
    return pl.pallas_call(
        attention_kernel,
        out_shape=[jax.ShapeDtypeStruct((2, TOK, 768), BF16)] * 4,
        grid_spec=grid_spec,
        compiler_params=params(),
        cost_estimate=pl.CostEstimate(
            flops=14 * 10**9,
            bytes_accessed=8 * 1024 * 1024,
            transcendentals=4 * 10 * 256 * 256,
        ),
    )(info, packed, packed, packed, mine, theirs, o_own, o_sib)


def merge_kernel(info, *refs):
    *near, far, queries, keys, values = refs
    here, core = info[0], info[3]
    for step in range(4):
        chip = lax.rem(here - step + 4, 4)
        mine, theirs = near[step][0], far[step]
        spot = chip * 1024 + core * 512
        queries[:, pl.ds(pl.multiple_of(spot, 512), 512)] = mine[:, :512]
        spot = chip * 1024 + (1 - core) * 512
        queries[:, pl.ds(pl.multiple_of(spot, 512), 512)] = theirs[:, :512]
        both = mine[:, 512:].astype(F32) + theirs[:, 512:].astype(F32)
        spot = pl.ds(pl.multiple_of(chip * 128, 128), 128)
        keys[:, spot] = both[:, :128].astype(BF16)
        values[:, spot] = both[:, 128:].astype(BF16)


def merge(info, near, far):
    whole = pl.BlockSpec(memory_space=pltpu.VMEM)
    return pl.pallas_call(
        merge_kernel,
        out_shape=(
            jax.ShapeDtypeStruct((TOK, 4096), BF16),
            jax.ShapeDtypeStruct((TOK, 512), BF16),
            jax.ShapeDtypeStruct((TOK, 512), BF16),
        ),
        in_specs=[pl.BlockSpec(memory_space=pltpu.SMEM)] + [whole] * 5,
        out_specs=(whole, whole, whole),
        compiler_params=params(),
    )(info, *near, far)


def add(*terms):
    total = terms[0].astype(F32)
    for term in terms[1:]:
        total = total + term.astype(F32)
    return total


def per_device(queries, keys, values, attn_out, out_grad, out_weight, lengths):
    x, core, y, z = (lax.axis_index(name) for name in ("x", "core", "y", "z"))
    info = jnp.stack([x, y, z, core]).astype(jnp.int32)
    info = jnp.concatenate([info, lengths[0]])
    factor = 32768 ** (-0.5)

    def halves(value):
        left, right = value[:, :2560], value[:, 2560:]
        return jnp.where(core == 0, left, right), jnp.where(core == 0, right, left)

    weight_mine, weight_theirs = halves(out_weight)
    weight_pair = jnp.stack([weight_mine, swap(weight_theirs)])
    near = jnp.stack([weight_pair] + [shift(weight_pair, "y", r) for r in (1, 2, 3)])

    o_split = jnp.transpose(attn_out.reshape(TOK, 4, 1024), (1, 0, 2))
    grad_mine, grad_theirs = halves(out_grad[0])
    own = (grad_mine, swap(grad_theirs))
    weight = lax.all_gather(after(near, o_split, grad_mine), "z", axis=0, tiled=False)
    o_own = lax.all_to_all(o_split, "x", split_axis=0, concat_axis=0, tiled=True)
    o_own = o_own.reshape(512, 1024)

    packed = jnp.concatenate(
        [
            queries.reshape(TOK, 8, 512),
            jnp.repeat(keys[0], 2, axis=1),
            jnp.repeat(values[0], 2, axis=1),
        ],
        axis=2,
    )
    packed = jnp.transpose(packed, (1, 0, 2))

    prev0, prev1 = (shift(part, "x", 1) for part in own)
    succ0, succ1 = (shift(part, "x", -1) for part in own)
    prev0, succ1, o_own = lax.optimization_barrier((prev0, succ1, o_own))
    packed = after(packed, prev0, succ1)
    packed = lax.all_to_all(packed, ("x", "core"), split_axis=0, concat_axis=0, tiled=True)
    packed = packed.reshape(1024, 768)
    o_sib = swap(o_own)
    far0, far1 = shift(prev0, "x", 1), shift(succ1, "x", -1)
    parts = (*own, prev0, prev1, succ0, succ1, far0, far1)
    term, rows = weight_product(info, parts, turn(o_own, o_sib), factor)

    summed = lax.psum_scatter(term, "z", scatter_dimension=0, tiled=True)[0]

    theirs = swap(project(info, rows, weight, 1, BF16))
    mine = project(info, rows, weight, 0, F32)
    grads = attention(info, packed, mine, theirs, o_own, o_sib)

    back = [grads[0]] + [shift(grads[r], "x", r) for r in (1, 2, 3)]
    grad_queries, grad_keys, grad_values = merge(
        info, back, swap(jnp.stack([part[1] for part in back]))
    )

    summed = after(summed, *back[1:])
    summed = [summed[0]] + [shift(summed[r], "y", r) for r in (1, 2, 3)]
    grad_queries = grad_queries.reshape(1, TOK, 32, 128)
    *summed, grad_queries, grad_keys, grad_values = lax.optimization_barrier(
        (*summed, grad_queries, grad_keys, grad_values)
    )
    summed = add(*summed)
    keep = jnp.where(core == 0, summed[0], summed[1])
    give = jnp.where(core == 0, summed[1], summed[0])
    come = swap(give)
    grad_out_weight = jnp.concatenate(
        [jnp.where(core == 0, keep, come), jnp.where(core == 0, come, keep)], axis=-1
    ).astype(F32)

    return (
        grad_queries,
        grad_keys.reshape(1, TOK, 4, 128),
        grad_values.reshape(1, TOK, 4, 128),
        grad_out_weight,
    )


def solution(mesh):
    mesh = Mesh(mesh.devices.reshape(4, 2, 4, 8), ("x", "core", "y", "z"))
    pack, token = ("y", "z"), ("x", "core")
    placed = (
        P(pack, token, None, None),
        P(pack, token, None, None),
        P(pack, token, None, None),
        P(pack, token, None, None),
        P(pack, token, None),
        P(token + pack, None),
        P(pack, None),
    )
    return jax.shard_map(
        per_device,
        mesh=mesh,
        in_specs=placed,
        out_specs=(
            P(pack, token, None, None),
            P(pack, token, None, None),
            P(pack, token, None, None),
            P(token + pack, None),
        ),
        check_vma=False,
    )
```
